32 devices in a mesh: seq: 4 (over y, x), batch: 8 (over z, core).
Axes of the slice: x: 2, y: 2, z: 4, core: 2. Of those that a mesh axis runs over, the one named last changes fastest.
Arguments:
- inputs: bfloat16 [24, 1024, 768], P('batch', 'seq'), may hold values from -6 to 6
- cotangent: bfloat16 [24, 1024, 768], P('batch', 'seq'), may hold values from -6 to 6
- lengths: int32 [24], P('batch'), may hold values from 1 to 1024, as said below
- query_weight: bfloat16 [768, 768], P(('seq', 'batch')), may hold values from -0.21875 to 0.21875
- query_bias: bfloat16 [768], P(('seq', 'batch')), may hold values from -3 to 3
- key_weight: bfloat16 [768, 768], P(('seq', 'batch')), may hold values from -0.21875 to 0.21875
- value_weight: bfloat16 [768, 768], P(('seq', 'batch')), may hold values from -0.21875 to 0.21875
- value_bias: bfloat16 [768], P(('seq', 'batch')), may hold values from -3 to 3
- out_weight: bfloat16 [768, 768], P(('seq', 'batch')), may hold values from -1.75 to 1.75
- out_bias: bfloat16 [768], P(('seq', 'batch')), may hold values from -3 to 3
- gain_one: bfloat16 [768], P(('seq', 'batch')), may hold values from 0.099609375 to 1.8984375
- shift_one: bfloat16 [768], P(('seq', 'batch')), may hold values from -3 to 3
- up_weight: bfloat16 [768, 3072], P(('seq', 'batch')), may hold values from -0.21875 to 0.21875
- up_bias: bfloat16 [3072], P(('seq', 'batch')), may hold values from -3 to 3
- down_weight: bfloat16 [3072, 768], P(('seq', 'batch')), may hold values from -0.109375 to 0.109375
- down_bias: bfloat16 [768], P(('seq', 'batch')), may hold values from -3 to 3
- gain_two: bfloat16 [768], P(('seq', 'batch')), may hold values from 0.099609375 to 1.8984375
- shift_two: bfloat16 [768], P(('seq', 'batch')), may hold values from -3 to 3
Outputs:
- output: bfloat16 [24, 1024, 768], P('batch', 'seq')
- input_grad: bfloat16 [24, 1024, 768], P('batch', 'seq')
- grad_query_weight: float32 [768, 768], P(('seq', 'batch'))
- grad_query_bias: float32 [768], P(('seq', 'batch'))
- grad_key_weight: float32 [768, 768], P(('seq', 'batch'))
- grad_value_weight: float32 [768, 768], P(('seq', 'batch'))
- grad_value_bias: float32 [768], P(('seq', 'batch'))
- grad_out_weight: float32 [768, 768], P(('seq', 'batch'))
- grad_out_bias: float32 [768], P(('seq', 'batch'))
- grad_gain_one: float32 [768], P(('seq', 'batch'))
- grad_shift_one: float32 [768], P(('seq', 'batch'))
- grad_up_weight: float32 [768, 3072], P(('seq', 'batch'))
- grad_up_bias: float32 [3072], P(('seq', 'batch'))
- grad_down_weight: float32 [3072, 768], P(('seq', 'batch'))
- grad_down_bias: float32 [768], P(('seq', 'batch'))
- grad_gain_two: float32 [768], P(('seq', 'batch'))
- grad_shift_two: float32 [768], P(('seq', 'batch'))
The draws below stay inside these ranges and needn't reach their ends.
Inputs may be any that keep to these rules, and one draw needn't show every extreme that they name: `lengths`: every batch index's 3 sequences include one of full length 1024.
All inputs are finite; a program needn't handle non-finite values.
Results may differ from the reference program's by a relative error of at most 0.015.
Values may be sent and summed in bfloat16 or wider, within the bound.
No kernel may reach another device: no remote copies, remote signals or barrier semaphores. Data moves between devices by JAX's collectives and lax.ppermute only.
A program may use at most 192 MiB of HBM per device.

```python
import jax
import jax.numpy as jnp
from jax import lax

D = 768
HEADS = 12
HEAD = 64
FF = 3072
SEQS = 3
LENGTH = 1024
SEQUENCES = 24


def draw_lengths(key, part):
    key = jax.random.fold_in(key, 11)
    key_one, key_two = jax.random.split(key)
    groups = SEQUENCES // SEQS
    drawn_counts = jax.random.randint(key_one, (groups, SEQS), 1, LENGTH + 1)
    chosen = jax.random.randint(key_two, (groups, 1), 0, SEQS)
    column = jnp.arange(SEQS, dtype=jnp.int32)[None, :]
    drawn_counts = jnp.where(column == chosen, LENGTH, drawn_counts)
    return drawn_counts.reshape(groups * SEQS).astype(jnp.int32)


def levels(rng, extent, shards, smallest, top_value):
    loudness, own = 1.0, jax.random.fold_in(rng, 6)
    for axis_at, parts in shards:
        heights = jnp.exp(jax.random.uniform(jax.random.fold_in(own, axis_at), (parts,), jnp.float32, smallest / len(shards), top_value / len(shards)))
        loudness = loudness * jnp.repeat(heights, extent[axis_at] // parts).reshape([-1 if axis == axis_at else 1 for axis in range(len(extent))])
    return loudness


def noise(own_key, dims, spread, reach, shards=(), kind=jnp.bfloat16):
    array = jax.random.normal(own_key, dims, jnp.float32) * spread
    if len(shards) > 0:
        array = levels(own_key, dims, shards, -0.22, 0.18) * array
    return jnp.clip(array, min=-reach, max=reach).astype(kind)


def setup_inputs(seed: int = 0) -> dict:
    arg_keys = jax.random.split(jax.random.key(seed), 19)
    inputs = noise(arg_keys[0], (SEQUENCES, LENGTH, D), 1.0, 6.0, ((0, 8), (1, 4)))
    cotangent = noise(arg_keys[1], (SEQUENCES, LENGTH, D), 1.0, 6.0, ((0, 8), (1, 4)))
    lengths = draw_lengths(jax.random.fold_in(arg_keys[18], 71), 0)
    query_weight = noise(arg_keys[3], (D, D), D ** -0.5, 0.21875, ((0, 32),))
    query_bias = noise(arg_keys[4], (D,), 0.5, 3.0, ((0, 32),))
    key_weight = noise(arg_keys[5], (D, D), D ** -0.5, 0.21875, ((0, 32),))
    value_weight = noise(arg_keys[6], (D, D), D ** -0.5, 0.21875, ((0, 32),))
    value_bias = noise(arg_keys[7], (D,), 0.5, 3.0, ((0, 32),))
    out_weight = noise(arg_keys[8], (D, D), (D // 64) ** -0.5, 1.75, ((0, 32),))
    out_bias = noise(arg_keys[9], (D,), 0.5, 3.0, ((0, 32),))
    gain_one = jnp.clip(1.0 + 0.18 * jax.random.normal(arg_keys[10], (D,), jnp.float32), 0.099609375, 1.8984375).astype(jnp.bfloat16)
    shift_one = noise(arg_keys[11], (D,), 0.5, 3.0, ((0, 32),))
    up_weight = noise(arg_keys[12], (D, FF), D ** -0.5, 0.21875, ((0, 32),))
    up_bias = noise(arg_keys[13], (FF,), 0.5, 3.0, ((0, 32),))
    down_weight = noise(arg_keys[14], (FF, D), FF ** -0.5, 0.109375, ((0, 32),))
    down_bias = noise(arg_keys[15], (D,), 0.5, 3.0, ((0, 32),))
    gain_two = jnp.clip(1.0 + 0.18 * jax.random.normal(arg_keys[16], (D,), jnp.float32), 0.099609375, 1.8984375).astype(jnp.bfloat16)
    shift_two = noise(arg_keys[17], (D,), 0.5, 3.0, ((0, 32),))
    return {"inputs": inputs, "cotangent": cotangent, "lengths": lengths, "query_weight": query_weight, "query_bias": query_bias, "key_weight": key_weight, "value_weight": value_weight, "value_bias": value_bias, "out_weight": out_weight, "out_bias": out_bias, "gain_one": gain_one, "shift_one": shift_one, "up_weight": up_weight, "up_bias": up_bias, "down_weight": down_weight, "down_bias": down_bias, "gain_two": gain_two, "shift_two": shift_two}


@jax.custom_vjp
def low(v):
    return lax.optimization_barrier(v.astype(jnp.bfloat16)).astype(jnp.float32)

@jax.custom_vjp
def low_back(v):
    return v

def low_keep(v):
    return (low(v), None)

def low_pass(kept, grad):
    return (grad,)

def back_keep(v):
    return (v, None)

def back_low(kept, grad):
    return (low(grad),)
low.defvjp(low_keep, low_pass)
low_back.defvjp(back_keep, back_low)

def matmul(left_side, right_side):
    return jnp.dot(left_side, right_side, precision=lax.Precision.HIGHEST)

def layer_norm(row_values, gain_vector, shift_vector):
    row_mean = lax.optimization_barrier(jnp.mean(row_values, axis=-1, keepdims=True))
    centred = row_values - row_mean
    row_var = lax.optimization_barrier(jnp.mean(centred * centred, axis=-1, keepdims=True))
    return centred * lax.rsqrt(row_var + 1e-05) * gain_vector + shift_vector

def forward_seq(tokens_in, valid_keys, params):
    query_weight, query_bias, key_weight, value_weight, value_bias, out_weight, out_bias, gain_one, shift_one, up_weight, up_bias, down_weight, down_bias, gain_two, shift_two = params
    row_count = tokens_in.shape[0]
    query_rows = low(low_back(matmul(tokens_in, query_weight) + query_bias)).reshape(row_count, HEADS, HEAD)
    key_rows = low(low_back(matmul(tokens_in, key_weight))).reshape(row_count, HEADS, HEAD)
    value_rows = low(low_back(matmul(tokens_in, value_weight) + value_bias)).reshape(row_count, HEADS, HEAD)
    raw_scores = low_back(jnp.einsum('ihd,jhd->hij', query_rows, key_rows, precision=lax.Precision.HIGHEST))
    scores = jnp.where(valid_keys[None, None, :], 0.125 * raw_scores, -1e+30)
    top_score = lax.optimization_barrier(jnp.max(scores, axis=-1, keepdims=True))
    exp_terms = jnp.exp(scores - top_score)
    attention_weights = exp_terms / lax.optimization_barrier(jnp.sum(exp_terms, axis=-1, keepdims=True))
    mixed = jnp.einsum('hij,jhd->ihd', low(attention_weights), value_rows, precision=lax.Precision.HIGHEST)
    mixed = low(low_back(mixed)).reshape(row_count, HEADS * HEAD)
    attended = low_back(matmul(mixed, out_weight) + out_bias)
    hidden = layer_norm(tokens_in + attended, gain_one, shift_one)
    up_values = low_back(matmul(low(hidden), up_weight) + up_bias)
    active = low(jax.nn.gelu(up_values, approximate=True))
    down_values = low_back(matmul(active, down_weight) + down_bias)
    return layer_norm(hidden + down_values, gain_two, shift_two)

def add_pair(earlier_sum, new_term):
    return earlier_sum + new_term

def reference(inputs, cotangent, lengths, query_weight, query_bias, key_weight, value_weight, value_bias, out_weight, out_bias, gain_one, shift_one, up_weight, up_bias, down_weight, down_bias, gain_two, shift_two):
    params = tuple((weight_arg.astype(jnp.float32) for weight_arg in (query_weight, query_bias, key_weight, value_weight, value_bias, out_weight, out_bias, gain_one, shift_one, up_weight, up_bias, down_weight, down_bias, gain_two, shift_two)))
    seqs_in = inputs.astype(jnp.float32)
    cot_in = cotangent.astype(jnp.float32)
    positions = jnp.arange(LENGTH, dtype=jnp.int32)

    def step_seq(totals, scanned):
        tokens_in, cot_seq, length_one = scanned
        valid_keys = positions < length_one

        def apply_layer(tokens_arg, params_arg):
            return forward_seq(tokens_arg, valid_keys, params_arg)
        result, pull_back = jax.vjp(apply_layer, tokens_in, params)
        grad_tokens, grad_params = pull_back(cot_seq)
        totals = jax.tree.map(add_pair, totals, grad_params)
        return (totals, (result, grad_tokens))
    zero_grads = jax.tree.map(jnp.zeros_like, params)
    totals, (results, grad_inputs) = lax.scan(step_seq, zero_grads, (seqs_in, cot_in, lengths.astype(jnp.int32)))
    grad_query_weight, grad_query_bias, grad_key_weight, grad_value_weight, grad_value_bias, grad_out_weight, grad_out_bias, grad_gain_one, grad_shift_one, grad_up_weight, grad_up_bias, grad_down_weight, grad_down_bias, grad_gain_two, grad_shift_two = totals
    return (results.astype(jnp.bfloat16), grad_inputs.astype(jnp.bfloat16), grad_query_weight, grad_query_bias, grad_key_weight, grad_value_weight, grad_value_bias, grad_out_weight, grad_out_bias, grad_gain_one, grad_shift_one, grad_up_weight, grad_up_bias, grad_down_weight, grad_down_bias, grad_gain_two, grad_shift_two)
```

```python
from functools import partial

import jax
import jax.numpy as jnp
from jax import lax
from jax.experimental import pallas as pl
from jax.experimental.pallas import tpu as pltpu
from jax.sharding import Mesh
from jax.sharding import PartitionSpec as P

HEAD = 64
LANES = 256
SCALE = 0.125
LOG2E = 1.4426950408889634
NEG = -1e30
VMEM_LIMIT = 56 * 1024 * 1024


def nt_dot(left, right):
    return lax.dot_general(left, right, (((1,), (1,)), ((), ())), preferred_element_type=jnp.float32)


def tn_dot(left, right):
    return lax.dot_general(left, right, (((0,), (0,)), ((), ())), preferred_element_type=jnp.float32)


def nn_dot(left, right):
    return jnp.dot(left, right, preferred_element_type=jnp.float32)


def attend_kernel(heads, q_ref, k_ref, v_ref, o_ref, stat_ref):
    lane = lax.broadcasted_iota(jnp.int32, (1, LANES), 1)
    width = heads * HEAD
    q = q_ref[...]
    rows = q.shape[0]
    total = jnp.zeros((rows, LANES), jnp.float32)
    stat = jnp.zeros((rows, 128), jnp.float32)
    lane_stat = lax.broadcasted_iota(jnp.int32, (1, 128), 1)
    for h in range(heads):
        own = lane // HEAD == h
        qh = jnp.where(own | (lane == width), q, jnp.zeros_like(q))
        s = nt_dot(qh, k_ref[...])
        top = jnp.max(s, axis=1, keepdims=True)
        p = jnp.exp2((s - top) * (SCALE * LOG2E))
        o = nn_dot(p.astype(jnp.bfloat16), v_ref[...])
        norm = o[:, width : width + 1]
        total = jnp.where(own, o * (1.0 / norm), total)
        stat = jnp.where(lane_stat == h, top * (SCALE * LOG2E) + jnp.log2(norm), stat)
    o_ref[...] = total[:, :width]
    stat_ref[...] = stat


def attend(qkv, heads):
    length = qkv.shape[0]
    block = 256
    width = heads * HEAD
    return pl.pallas_call(
        partial(attend_kernel, heads),
        grid=(length // block,),
        in_specs=[
            pl.BlockSpec((block, LANES), lambda i: (i, 0)),
            pl.BlockSpec((length, LANES), lambda i: (0, 1)),
            pl.BlockSpec((length, LANES), lambda i: (0, 2)),
        ],
        out_specs=[
            pl.BlockSpec((block, width), lambda i: (i, 0)),
            pl.BlockSpec((block, 128), lambda i: (i, 0)),
        ],
        out_shape=[
            jax.ShapeDtypeStruct((length, width), jnp.float32),
            jax.ShapeDtypeStruct((length, 128), jnp.float32),
        ],
        compiler_params=pltpu.CompilerParams(vmem_limit_bytes=VMEM_LIMIT),
        cost_estimate=pl.CostEstimate(
            flops=4 * heads * length * length * LANES, bytes_accessed=8 * length * LANES,
            transcendentals=heads * length * length,
        ),
        name="attend",
    )(qkv, qkv, qkv)


def attend_back_kernel(heads, block, qkv_ref, o_ref, do_ref, stat_ref, out_ref, dq_ref, rows_ref):
    length = qkv_ref.shape[0]
    width = heads * HEAD
    lane = lax.broadcasted_iota(jnp.int32, (1, LANES), 1)
    lane_w = lax.broadcasted_iota(jnp.int32, (1, width), 1)
    lane_stat = lax.broadcasted_iota(jnp.int32, (1, 128), 1)
    do = do_ref[...]
    prod = do.astype(jnp.float32) * o_ref[...]
    stat = stat_ref[...]
    for h in range(heads):
        delta = jnp.sum(jnp.where(lane_w // HEAD == h, prod, 0.0), axis=1, keepdims=True)
        stat = jnp.where(lane_stat == heads + h, delta, stat)
    rows_ref[...] = jnp.transpose(stat)
    dq_ref[...] = jnp.zeros_like(dq_ref)

    def step(kb, carry):
        start = pl.multiple_of(kb * block, block)
        kblk = qkv_ref[pl.ds(start, block), LANES : 2 * LANES]
        vblk = qkv_ref[pl.ds(start, block), 2 * LANES : 2 * LANES + width]
        dk = jnp.zeros((block, LANES), jnp.float32)
        dv = jnp.zeros((block, width), jnp.float32)
        for h in range(heads):
            own = lane // HEAD == h
            own_w = lane_w // HEAD == h
            kh = jnp.where(own, kblk, jnp.zeros_like(kblk))
            kh_mask = jnp.where(own | (lane == width), kblk, jnp.zeros_like(kblk))
            vh = jnp.where(own_w, vblk, jnp.zeros_like(vblk))
            s = nt_dot(kh_mask, qkv_ref[:, 0:LANES])
            p = jnp.exp2(s * (SCALE * LOG2E) - rows_ref[h : h + 1, :])
            dp = nt_dot(vh, do_ref[...])
            ds = (p * (dp - rows_ref[heads + h : heads + h + 1, :])).astype(jnp.bfloat16)
            dv = jnp.where(own_w, nn_dot(p.astype(jnp.bfloat16), do_ref[...]), dv)
            dk = jnp.where(own, nn_dot(ds, qkv_ref[:, 0:LANES]), dk)
            dq_ref[...] += tn_dot(ds, kh)
        out_ref[pl.ds(start, block), LANES : 2 * LANES] = (dk * SCALE).astype(jnp.bfloat16)
        out_ref[pl.ds(start, block), 2 * LANES : 2 * LANES + width] = dv.astype(jnp.bfloat16)
        out_ref[pl.ds(start, block), 2 * LANES + width :] = jnp.zeros(
            (block, LANES - width), jnp.bfloat16
        )
        return carry

    lax.fori_loop(0, length // block, step, 0)
    out_ref[:, 0:LANES] = (dq_ref[...] * SCALE).astype(jnp.bfloat16)


def attend_back(qkv, o, do, stat, heads):
    length = qkv.shape[0]
    vmem = pl.BlockSpec(memory_space=pltpu.VMEM)
    return pl.pallas_call(
        partial(attend_back_kernel, heads, 256),
        in_specs=[vmem] * 4,
        out_specs=vmem,
        out_shape=jax.ShapeDtypeStruct((length, 3 * LANES), jnp.bfloat16),
        scratch_shapes=[
            pltpu.VMEM((length, LANES), jnp.float32),
            pltpu.VMEM((128, length), jnp.float32),
        ],
        compiler_params=pltpu.CompilerParams(vmem_limit_bytes=VMEM_LIMIT),
        cost_estimate=pl.CostEstimate(
            flops=10 * heads * length * length * LANES, bytes_accessed=16 * length * LANES,
            transcendentals=heads * length * length,
        ),
        name="attend_back",
    )(qkv, o, do, stat)


def layer_norm(row_values, gain_vector, shift_vector):
    row_mean = jnp.mean(row_values, axis=-1, keepdims=True)
    centred = row_values - row_mean
    row_var = jnp.mean(centred * centred, axis=-1, keepdims=True)
    return centred * lax.rsqrt(row_var + 1e-05) * gain_vector + shift_vector


def gelu_tanh(up_values):
    return jax.nn.gelu(up_values, approximate=True)


def body(
    inputs,
    cotangent,
    lengths,
    query_weight,
    query_bias,
    key_weight,
    value_weight,
    value_bias,
    out_weight,
    out_bias,
    gain_one,
    shift_one,
    up_weight,
    up_bias,
    down_weight,
    down_bias,
    gain_two,
    shift_two,
):
    bf = jnp.bfloat16
    seqs, rows, width = inputs.shape
    ns, nz, nc = lax.axis_size("seq"), lax.axis_size("zz"), lax.axis_size("core")
    nb = nz * nc
    n = ns * nb
    every = ("seq", "zz", "core")
    me = lax.axis_index("seq")
    core = lax.axis_index("core")
    length = rows * ns
    tokens = seqs * rows
    wr = query_weight.shape[0]
    ff = up_weight.shape[1]
    chunks = ff // width
    hw = width // ns
    heads = hw // HEAD

    def swap(a, bit):
        return lax.ppermute(a, "seq", [(i, i ^ bit) for i in range(ns)])

    qkv_cols = jnp.concatenate(
        [w.reshape(wr, ns, hw).transpose(1, 0, 2) for w in (query_weight, key_weight, value_weight)], axis=2
    )
    bias_row = jnp.concatenate([query_bias, value_bias, jnp.zeros((3 * hw - 2 * wr,), bf)])
    pad_w = -(wr + 1) % 8
    to_each = jnp.concatenate(
        [
            qkv_cols,
            jnp.broadcast_to(bias_row[None, None], (ns, 1, 3 * hw)),
            jnp.zeros((ns, pad_w, 3 * hw), bf),
        ],
        axis=1,
    )
    to_each = jnp.broadcast_to(to_each[:, None], (ns, nb, wr + 1 + pad_w, 3 * hw)).reshape(
        n, wr + 1 + pad_w, 3 * hw
    )
    got = lax.all_to_all(to_each, every, 0, 0, tiled=True)
    weight_qkv = got[:, :wr].reshape(width, 3, hw)
    weight_qkv = jnp.pad(weight_qkv, ((0, 0), (0, 0), (0, LANES - hw))).reshape(width, 3 * LANES)
    bias_mine = lax.dynamic_slice_in_dim(got[:, wr], me * nb, nb, 0)
    ones = jnp.ones((LANES - hw,), bf)
    bias_qkv = jnp.concatenate(
        [
            bias_mine[:, :wr].reshape(hw),
            ones,
            jnp.zeros((LANES,), bf),
            bias_mine[:, wr : 2 * wr].reshape(hw),
            ones,
        ]
    ).astype(jnp.float32)

    vectors = jnp.concatenate([out_bias, gain_one, shift_one, down_bias, gain_two, shift_two, up_bias])
    vectors = jnp.pad(vectors, (0, width - vectors.shape[0]))[None]
    r_out, r_up, r_down = wr, chunks * wr, down_weight.shape[0]
    r_vec = r_out + r_up + r_down
    r_all = r_vec + 1 + (-(r_vec + 1) % 8)
    packed = jnp.concatenate(
        [
            out_weight,
            up_weight.reshape(wr, chunks, width).transpose(1, 0, 2).reshape(r_up, width),
            down_weight,
            vectors,
            jnp.zeros((r_all - r_vec - 1, width), bf),
        ],
        axis=0,
    )
    gathered = lax.all_gather(packed, every, axis=0, tiled=False)

    positions = jnp.arange(length, dtype=jnp.int32)
    col = jnp.arange(3 * LANES, dtype=jnp.int32)
    half = rows // 2
    seq_tokens, qkvs, mixes, stats, mixed_parts = [], [], [], [], []
    for j in range(seqs):
        own = inputs[j]
        by_one, by_two = swap(own, 1), swap(own, 2)
        top, bottom = swap(by_one[:half], 2), swap(by_two[half:], 1)
        whole = jnp.zeros((ns, rows, width), bf)
        whole = lax.dynamic_update_slice_in_dim(whole, own[None], me, 0)
        whole = lax.dynamic_update_slice_in_dim(whole, by_one[None], me ^ 1, 0)
        whole = lax.dynamic_update_slice_in_dim(whole, by_two[None], me ^ 2, 0)
        whole = lax.dynamic_update_slice(whole, top[None], (me ^ 3, 0, 0))
        whole = lax.dynamic_update_slice(whole, bottom[None], (me ^ 3, half, 0))
        whole = whole.reshape(length, width)
        qkv = (nn_dot(whole, weight_qkv) + bias_qkv).astype(bf)
        padding = jnp.where(positions < lengths[j], 0.0, NEG).astype(bf)
        qkv = jnp.where((col == LANES + hw)[None], padding[:, None], qkv)
        mix, stat = attend(qkv, heads)
        low = mix.astype(bf).reshape(ns, rows, hw)
        parts = jnp.zeros((ns, rows, hw), bf)
        for bit in range(ns):
            part = lax.dynamic_index_in_dim(low, me ^ bit, 0, keepdims=False)
            if bit:
                part = swap(part, bit)
            parts = lax.dynamic_update_slice_in_dim(parts, part[None], me ^ bit, 0)
        mixed_parts.append(parts.transpose(1, 0, 2).reshape(rows, width))
        seq_tokens.append(whole)
        qkvs.append(qkv)
        mixes.append(mix)
        stats.append(stat)

    whole_out = gathered[:, :r_out].reshape(width, width)
    whole_up = (
        gathered[:, r_out : r_out + r_up].reshape(n, chunks, wr, width).transpose(0, 2, 1, 3).reshape(width, ff)
    )
    whole_down = gathered[:, r_out + r_up : r_vec].reshape(ff, width)
    vecs = gathered[:, r_vec].astype(jnp.float32)
    six = vecs[:, : 6 * wr].reshape(n, 6, wr).transpose(1, 0, 2).reshape(6, width)
    bias_out, gain_first, shift_first, bias_down, gain_second, shift_second = (six[i] for i in range(6))
    bias_up = vecs[:, 6 * wr : 6 * wr + r_down].reshape(ff)

    input_block = inputs.reshape(tokens, width)
    cot_block = cotangent.reshape(tokens, width).astype(jnp.float32)
    mixed_low = jnp.concatenate(mixed_parts, axis=0)
    attended = nn_dot(mixed_low, whole_out) + bias_out
    hidden, norm_back_one = jax.vjp(
        layer_norm, input_block.astype(jnp.float32) + attended, gain_first, shift_first
    )
    hidden_low = hidden.astype(bf)
    up_values = nn_dot(hidden_low, whole_up) + bias_up
    active, gelu_back = jax.vjp(gelu_tanh, up_values)
    active_low = active.astype(bf)
    down_values = nn_dot(active_low, whole_down) + bias_down
    normed, norm_back_two = jax.vjp(layer_norm, hidden + down_values, gain_second, shift_second)
    output = normed.astype(bf).reshape(seqs, rows, width)
    grad_sum_two, grad_gain_two, grad_shift_two = norm_back_two(cot_block)
    grad_down_low = grad_sum_two.astype(bf)
    grad_down_weight = tn_dot(active_low, grad_down_low)
    grad_down_bias = jnp.sum(grad_down_low.astype(jnp.float32), axis=0)
    (grad_up,) = gelu_back(nt_dot(grad_down_low, whole_down))
    grad_up_low = grad_up.astype(bf)
    grad_up_weight = tn_dot(hidden_low, grad_up_low)
    grad_up_bias = jnp.sum(grad_up_low.astype(jnp.float32), axis=0)
    grad_hidden = grad_sum_two + nt_dot(grad_up_low, whole_up)
    grad_sum_one, grad_gain_one, grad_shift_one = norm_back_one(grad_hidden)
    grad_att_low = grad_sum_one.astype(bf)
    grad_out_weight = tn_dot(mixed_low, grad_att_low)
    grad_out_bias = jnp.sum(grad_att_low.astype(jnp.float32), axis=0)
    grad_mixed = nt_dot(grad_att_low, whole_out).astype(bf)

    vec_grads = jnp.stack(
        [grad_out_bias, grad_gain_one, grad_shift_one, grad_down_bias, grad_gain_two, grad_shift_two]
    )
    vec_grads = jnp.concatenate(
        [
            vec_grads.reshape(6, n, wr).transpose(1, 0, 2).reshape(n, 6 * wr),
            grad_up_bias.reshape(n, r_down),
            jnp.zeros((n, width - 6 * wr - r_down), jnp.float32),
        ],
        axis=1,
    )
    full = jnp.concatenate(
        [
            grad_out_weight.reshape(n, wr, width).astype(bf),
            grad_up_weight.astype(bf).reshape(n, wr, chunks, width).transpose(0, 2, 1, 3).reshape(n, r_up, width),
            grad_down_weight.reshape(n, r_down, width).astype(bf),
            vec_grads.astype(bf)[:, None],
            jnp.zeros((n, r_all - r_vec - 1, width), bf),
        ],
        axis=1,
    ).reshape(ns, nz, nc, r_all, width)
    theirs = lax.ppermute(
        lax.dynamic_index_in_dim(full, 1 - core, 2, keepdims=False), "core", [(0, 1), (1, 0)]
    )
    mine = lax.dynamic_index_in_dim(full, core, 2, keepdims=False)
    chip = (theirs.astype(jnp.float32) + mine.astype(jnp.float32)).astype(bf)
    shard = lax.psum_scatter(chip, "seq", scatter_dimension=0, tiled=False)
    shard = lax.psum_scatter(shard, "zz", scatter_dimension=0, tiled=False).astype(jnp.float32)

    back_blocks = grad_mixed.reshape(seqs, rows, ns, hw).transpose(0, 2, 1, 3)
    sum_qkv = jnp.zeros((width, 3 * LANES), jnp.float32)
    sum_bias = jnp.zeros((3 * LANES,), jnp.float32)
    grad_inputs = []
    for j in range(seqs):
        do = jnp.zeros((ns, rows, hw), bf)
        for bit in range(ns):
            part = lax.dynamic_index_in_dim(back_blocks[j], me ^ bit, 0, keepdims=False)
            if bit:
                part = swap(part, bit)
            do = lax.dynamic_update_slice_in_dim(do, part[None], me ^ bit, 0)
        grad_qkv = attend_back(qkvs[j], mixes[j], do.reshape(length, hw), stats[j], heads)
        sum_qkv = sum_qkv + tn_dot(seq_tokens[j], grad_qkv)
        sum_bias = sum_bias + jnp.sum(grad_qkv.astype(jnp.float32), axis=0)
        partial_x = nt_dot(grad_qkv, weight_qkv).astype(bf).reshape(ns, rows, width)
        acc = grad_sum_one[j * rows : (j + 1) * rows]
        for bit in range(ns):
            part = lax.dynamic_index_in_dim(partial_x, me ^ bit, 0, keepdims=False)
            if bit:
                part = swap(part, bit)
            acc = acc + part.astype(jnp.float32)
        grad_inputs.append(acc.astype(bf))
    grad_input = jnp.stack(grad_inputs)

    sum_qkv = sum_qkv.reshape(n, wr, 3, LANES)[..., :hw].reshape(n, wr, 3 * hw).astype(bf)
    bias_terms = jnp.concatenate(
        [sum_bias[:hw].reshape(nb, wr), sum_bias[2 * LANES : 2 * LANES + hw].reshape(nb, wr)], axis=1
    )
    bias_terms = jnp.pad(bias_terms, ((0, 0), (0, 3 * hw - 2 * wr))).astype(bf)
    bias_terms = jnp.broadcast_to(bias_terms[None], (ns, nb, 3 * hw)).reshape(n, 1, 3 * hw)
    back = jnp.concatenate([sum_qkv, bias_terms, jnp.zeros((n, pad_w, 3 * hw), bf)], axis=1)
    back = lax.all_to_all(back, every, 0, 0, tiled=True)
    back = jnp.sum(back.reshape(ns, nb, wr + 1 + pad_w, 3 * hw).astype(jnp.float32), axis=1)
    grads = back[:, :wr].reshape(ns, wr, 3, hw).transpose(2, 1, 0, 3).reshape(3, wr, width)
    bias_back = lax.dynamic_index_in_dim(back[:, wr], me, 0, keepdims=False)

    vec = shard[r_vec]
    out_g, gain1_g, shift1_g, downb_g, gain2_g, shift2_g = (vec[i * wr : (i + 1) * wr] for i in range(6))
    return (
        output,
        grad_input,
        grads[0],
        bias_back[:wr],
        grads[1],
        grads[2],
        bias_back[wr : 2 * wr],
        shard[:r_out],
        out_g,
        gain1_g,
        shift1_g,
        shard[r_out : r_out + r_up].reshape(chunks, wr, width).transpose(1, 0, 2).reshape(wr, ff),
        vec[6 * wr : 6 * wr + r_down],
        shard[r_out + r_up : r_vec],
        downb_g,
        gain2_g,
        shift2_g,
    )


def solution(mesh):
    sizes = mesh.shape
    cores = 2
    split = Mesh(
        mesh.devices.reshape(sizes["seq"], sizes["batch"] // cores, cores), ("seq", "zz", "core")
    )
    batch = ("zz", "core")
    every = ("seq", "zz", "core")
    tokens, matrix, vector = P(batch, "seq", None), P(every, None), P(every)
    return jax.shard_map(
        body,
        mesh=split,
        in_specs=(
            tokens, tokens, P(batch), matrix, vector, matrix, matrix, vector, matrix, vector,
            vector, vector, matrix, vector, matrix, vector, vector, vector,
        ),
        out_specs=(
            tokens, tokens, matrix, vector, matrix, matrix, vector, matrix, vector, vector,
            vector, matrix, vector, matrix, vector, vector, vector,
        ),
        check_vma=False,
    )
```

```python
from functools import partial

import jax
import jax.numpy as jnp
from jax import lax
from jax.experimental import pallas as pl
from jax.experimental.pallas import tpu as pltpu
from jax.sharding import Mesh
from jax.sharding import PartitionSpec as P

HEAD = 64
LANES = 256
SCALE = 0.125
LOG2E = 1.4426950408889634
NEG = -1e30
VMEM_LIMIT = 56 * 1024 * 1024


def nt_dot(left, right):
    return lax.dot_general(left, right, (((1,), (1,)), ((), ())), preferred_element_type=jnp.float32)


def tn_dot(left, right):
    return lax.dot_general(left, right, (((0,), (0,)), ((), ())), preferred_element_type=jnp.float32)


def nn_dot(left, right):
    return jnp.dot(left, right, preferred_element_type=jnp.float32)


def attend_kernel(heads, q_ref, k_ref, v_ref, *rest):
    o_ref, stat_ref = rest[-2:]
    lane = lax.broadcasted_iota(jnp.int32, (1, LANES), 1)
    width = heads * HEAD
    q = q_ref[...]
    rows = q.shape[0]
    total = jnp.zeros((rows, LANES), jnp.float32)
    stat = jnp.zeros((rows, 128), jnp.float32)
    lane_stat = lax.broadcasted_iota(jnp.int32, (1, 128), 1)
    for h in range(heads):
        own = lane // HEAD == h
        qh = jnp.where(own | (lane == width), q, jnp.zeros_like(q))
        s = nt_dot(qh, k_ref[...])
        top = jnp.max(s, axis=1, keepdims=True)
        p = jnp.exp2((s - top) * (SCALE * LOG2E))
        o = nn_dot(p.astype(jnp.bfloat16), v_ref[...])
        norm = o[:, width : width + 1]
        total = jnp.where(own, o * (1.0 / norm), total)
        stat = jnp.where(lane_stat == h, top * (SCALE * LOG2E) + jnp.log2(norm), stat)
    o_ref[...] = total[:, :width]
    stat_ref[...] = stat


def attend(qkv, heads, deps):
    length = qkv.shape[0]
    block = 256
    width = heads * HEAD
    return pl.pallas_call(
        partial(attend_kernel, heads),
        grid=(length // block,),
        in_specs=[
            pl.BlockSpec((block, LANES), lambda i: (i, 0)),
            pl.BlockSpec((length, LANES), lambda i: (0, 1)),
            pl.BlockSpec((length, LANES), lambda i: (0, 2)),
        ]
        + [pl.BlockSpec(memory_space=pl.ANY)] * len(deps),
        out_specs=[
            pl.BlockSpec((block, width), lambda i: (i, 0)),
            pl.BlockSpec((block, 128), lambda i: (i, 0)),
        ],
        out_shape=[
            jax.ShapeDtypeStruct((length, width), jnp.float32),
            jax.ShapeDtypeStruct((length, 128), jnp.float32),
        ],
        compiler_params=pltpu.CompilerParams(vmem_limit_bytes=VMEM_LIMIT),
        cost_estimate=pl.CostEstimate(
            flops=4 * heads * length * length * LANES, bytes_accessed=8 * length * LANES,
            transcendentals=heads * length * length,
        ),
        name="attend",
    )(qkv, qkv, qkv, *deps)


def attend_back_kernel(heads, block, qkv_ref, o_ref, do_ref, stat_ref, *rest):
    out_ref, dq_ref, rows_ref = rest[-3:]
    length = qkv_ref.shape[0]
    width = heads * HEAD
    lane = lax.broadcasted_iota(jnp.int32, (1, LANES), 1)
    lane_w = lax.broadcasted_iota(jnp.int32, (1, width), 1)
    lane_stat = lax.broadcasted_iota(jnp.int32, (1, 128), 1)
    do = do_ref[...]
    prod = do.astype(jnp.float32) * o_ref[...]
    stat = stat_ref[...]
    for h in range(heads):
        delta = jnp.sum(jnp.where(lane_w // HEAD == h, prod, 0.0), axis=1, keepdims=True)
        stat = jnp.where(lane_stat == heads + h, delta, stat)
    rows_ref[...] = jnp.transpose(stat)
    dq_ref[...] = jnp.zeros_like(dq_ref)

    def step(kb, carry):
        start = pl.multiple_of(kb * block, block)
        kblk = qkv_ref[pl.ds(start, block), LANES : 2 * LANES]
        vblk = qkv_ref[pl.ds(start, block), 2 * LANES : 2 * LANES + width]
        dk = jnp.zeros((block, LANES), jnp.float32)
        dv = jnp.zeros((block, width), jnp.float32)
        for h in range(heads):
            own = lane // HEAD == h
            own_w = lane_w // HEAD == h
            kh = jnp.where(own, kblk, jnp.zeros_like(kblk))
            kh_mask = jnp.where(own | (lane == width), kblk, jnp.zeros_like(kblk))
            vh = jnp.where(own_w, vblk, jnp.zeros_like(vblk))
            s = nt_dot(kh_mask, qkv_ref[:, 0:LANES])
            p = jnp.exp2(s * (SCALE * LOG2E) - rows_ref[h : h + 1, :])
            dp = nt_dot(vh, do_ref[...])
            ds = (p * (dp - rows_ref[heads + h : heads + h + 1, :])).astype(jnp.bfloat16)
            dv = jnp.where(own_w, nn_dot(p.astype(jnp.bfloat16), do_ref[...]), dv)
            dk = jnp.where(own, nn_dot(ds, qkv_ref[:, 0:LANES]), dk)
            dq_ref[...] += tn_dot(ds, kh)
        out_ref[pl.ds(start, block), LANES : 2 * LANES] = (dk * SCALE).astype(jnp.bfloat16)
        out_ref[pl.ds(start, block), 2 * LANES : 2 * LANES + width] = dv.astype(jnp.bfloat16)
        out_ref[pl.ds(start, block), 2 * LANES + width :] = jnp.zeros(
            (block, LANES - width), jnp.bfloat16
        )
        return carry

    lax.fori_loop(0, length // block, step, 0)
    out_ref[:, 0:LANES] = (dq_ref[...] * SCALE).astype(jnp.bfloat16)


def attend_back(qkv, o, do, stat, heads, deps):
    length = qkv.shape[0]
    vmem = pl.BlockSpec(memory_space=pltpu.VMEM)
    return pl.pallas_call(
        partial(attend_back_kernel, heads, 256),
        in_specs=[vmem] * 4 + [pl.BlockSpec(memory_space=pl.ANY)] * len(deps),
        out_specs=vmem,
        out_shape=jax.ShapeDtypeStruct((length, 3 * LANES), jnp.bfloat16),
        scratch_shapes=[
            pltpu.VMEM((length, LANES), jnp.float32),
            pltpu.VMEM((128, length), jnp.float32),
        ],
        compiler_params=pltpu.CompilerParams(vmem_limit_bytes=VMEM_LIMIT),
        cost_estimate=pl.CostEstimate(
            flops=10 * heads * length * length * LANES, bytes_accessed=16 * length * LANES,
            transcendentals=heads * length * length,
        ),
        name="attend_back",
    )(qkv, o, do, stat, *deps)


def weight_copies(places, refs, wd_ref, wu_ref, wo_ref, sem_ref):
    if places is None:
        pairs = list(zip(refs, [ref for ref in (wd_ref, wu_ref, wo_ref) if ref is not None]))
        return [pltpu.make_async_copy(a, d, sem_ref.at[q]) for q, (a, d) in enumerate(pairs)]
    me, core = lax.axis_index("seq"), lax.axis_index("core")
    rows_up, lanes = wo_ref.shape[2], wo_ref.shape[3] // 2
    cut = rows_up * 2 // 3
    pairs = []
    for p, (b, z) in enumerate(places):
        for k in range(2):
            src = refs[2 * p + k]
            base = src.shape[1] - cut
            down = base - 2 * rows_up
            c = core if k == 0 else 1 - core
            zs = pl.ds(z, src.shape[0])
            at = pl.multiple_of(c * lanes, 128)
            if wd_ref is not None:
                pairs.append((src.at[:, pl.ds(0, down)], wd_ref.at[me ^ b, zs, c]))
            pairs += [
                (src.at[:, pl.ds(down, rows_up)], wu_ref.at[2 * c, me ^ b, zs]),
                (src.at[:, pl.ds(down + rows_up, rows_up)], wu_ref.at[2 * c + 1, me ^ b, zs]),
                (
                    src.at[:, pl.ds(base, cut), pl.ds(0, lanes)],
                    wo_ref.at[b, zs, pl.ds(0, cut), pl.ds(at, lanes)],
                ),
                (
                    src.at[:, pl.ds(base, rows_up - cut), pl.ds(lanes, lanes)],
                    wo_ref.at[b, zs, pl.ds(cut, rows_up - cut), pl.ds(at, lanes)],
                ),
            ]
    return [pltpu.make_async_copy(a, d, sem_ref.at[q]) for q, (a, d) in enumerate(pairs)]


def weight_scratch(sizes, width, chunks, with_down):
    bf = jnp.bfloat16
    if sizes is None:
        shapes = [(chunks, width, width), (chunks, width, width), (width, width)]
    else:
        ns, nz, nc, rd, pair = sizes
        shapes = [(ns, nz, nc, rd, width), (chunks, ns, nz, pair, width), (ns, nz, pair, width)]
    return [pltpu.VMEM(s, bf) for s in shapes[0 if with_down else 1 :]] + [pltpu.SemaphoreType.DMA((64,))]


ANY = pl.BlockSpec(memory_space=pl.ANY)


def normalise(r):
    mean = jnp.mean(r, axis=-1, keepdims=True)
    centred = r - mean
    rstd = lax.rsqrt(jnp.mean(centred * centred, axis=-1, keepdims=True) + 1e-05)
    return centred * rstd, rstd


def norm_back(e, n, rstd):
    return rstd * (e - jnp.mean(e, axis=-1, keepdims=True) - n * jnp.mean(e * n, axis=-1, keepdims=True))


GELU_A = 0.7978845608028654
GELU_B = 0.044715


def gelu_both(u):
    sq = u * u
    t = jnp.tanh(u * (GELU_A + (GELU_A * GELU_B) * sq))
    half = 0.5 * (1.0 + t)
    slope = half + (0.5 * u) * (1.0 - t * t) * (GELU_A + (3.0 * GELU_A * GELU_B) * sq)
    return u * half, slope


def ffn_kernel(
    places, given, x_ref, mixed_ref, cot_ref, vec_ref, *rest
):
    split = places is not None
    weights, (out_ref, sum2_ref, n1_ref, rstd1_ref, hid_ref, gup_ref, *rest) = rest[:given], rest[given:]
    *rest, wd_ref, wu_ref, wo_ref, load_ref = rest
    if split:
        mine_ref, theirs_ref, vsum_ref, act_ref, gdl_ref, slope_ref, stage_ref, sem_ref = rest
    else:
        dwd_ref, vsum_ref, act_ref, gdl_ref, slope_ref = rest
    bf = jnp.bfloat16
    i = pl.program_id(0)
    rows, width = x_ref.shape
    chunks = wu_ref.shape[0]

    @pl.when(i == 0)
    def _():
        copies = weight_copies(places, weights, wd_ref, wu_ref, wo_ref, load_ref)
        for copy in copies:
            copy.start()
        for copy in copies:
            copy.wait()

    def wu(j):
        return wu_ref[j].reshape(width, width)

    def wd(j):
        return wd_ref[j].reshape(width, width)

    vec = vec_ref[...]
    r = x_ref[...].astype(jnp.float32) + nn_dot(mixed_ref[...], wo_ref[...].reshape(width, width)) + vec[0:1]
    n1, rstd1 = normalise(r)
    n1_ref[...] = n1
    rstd1_ref[...] = jnp.broadcast_to(rstd1, rstd1_ref.shape)
    hidden = n1 * vec[1:2] + vec[2:3]
    hid_low = hidden.astype(bf)
    hid_ref[...] = hid_low
    mine = pl.ds(pl.multiple_of(i * rows, rows), rows)
    down = hidden + vec[3:4]
    for j in range(chunks):
        active, slope = gelu_both(nn_dot(hid_low, wu(j)) + vec[6 + j : 7 + j])
        slope_ref[j] = slope
        low = active.astype(bf)
        act_ref[j, mine, :] = low
        down = down + nn_dot(low, wd(j))
    n2, rstd2 = normalise(down)
    out_ref[...] = (n2 * vec[4:5] + vec[5:6]).astype(bf)
    cot = cot_ref[...].astype(jnp.float32)
    sum2 = norm_back(cot * vec[4:5], n2, rstd2)
    sum2_ref[...] = sum2
    gdl = sum2.astype(bf)
    gdl_ref[mine, :] = gdl
    sums = [
        jnp.sum(gdl.astype(jnp.float32), axis=0, keepdims=True),
        jnp.sum(cot * n2, axis=0, keepdims=True),
        jnp.sum(cot, axis=0, keepdims=True),
        jnp.zeros((1, width), jnp.float32),
    ]
    for j in range(chunks):
        gup = (nt_dot(gdl, wd(j)) * slope_ref[j]).astype(bf)
        gup_ref[j] = gup
        sums.append(jnp.sum(gup.astype(jnp.float32), axis=0, keepdims=True))
    sums = jnp.concatenate(sums, axis=0)

    @pl.when(i == 0)
    def _():
        vsum_ref[...] = sums

    @pl.when(i > 0)
    def _():
        vsum_ref[...] += sums

    @pl.when(i == pl.num_programs(0) - 1)
    def _():
        copies = []
        for j in range(chunks):
            grad = tn_dot(act_ref[j], gdl_ref[...]).astype(bf)
            if not split:
                dwd_ref[j] = grad
                continue
            stage_ref[j] = grad.reshape(stage_ref.shape[1:])
            me, core = lax.axis_index("seq"), lax.axis_index("core")
            for k, (dst_ref, half) in enumerate(((mine_ref, core), (theirs_ref, 1 - core))):
                copy = pltpu.make_async_copy(
                    stage_ref.at[j, :, half], dst_ref.at[me ^ j], sem_ref.at[j, k]
                )
                copy.start()
                copies.append(copy)
        for copy in copies:
            copy.wait()


def const_spec(shape):
    return pl.BlockSpec(shape, lambda i: (0,) * len(shape), pipeline_mode=pl.Buffered(1))


def ffn(x, mixed, cot, vec, weights, places, sizes, rows, chunks, deps):
    bf = jnp.bfloat16
    tokens, width = x.shape
    block = pl.BlockSpec((rows, width), lambda i: (i, 0))
    if sizes:
        ns, nz, nc, wr, _ = sizes
        half = (ns, nz, wr, width)
        grad_specs = [pl.BlockSpec(memory_space=pl.ANY)] * 2
        grad_shapes = [jax.ShapeDtypeStruct(half, bf)] * 2
        grad_scratch = [
            pltpu.VMEM((chunks, nz, nc, wr, width), bf),
            pltpu.SemaphoreType.DMA((chunks, 2)),
        ]
    else:
        whole = (chunks, width, width)
        grad_specs, grad_shapes = [const_spec(whole)], [jax.ShapeDtypeStruct(whole, bf)]
        grad_scratch = []
    return pl.pallas_call(
        partial(ffn_kernel, places, len(weights) + len(deps)),
        grid=(tokens // rows,),
        in_specs=[block, block, block, const_spec(vec.shape)] + [ANY] * (len(weights) + len(deps)),
        out_specs=[
            block,
            block,
            block,
            pl.BlockSpec((rows, 128), lambda i: (i, 0)),
            block,
            pl.BlockSpec((chunks, rows, width), lambda i: (0, i, 0)),
            *grad_specs,
            const_spec((4 + chunks, width)),
        ],
        out_shape=[
            jax.ShapeDtypeStruct((tokens, width), bf),
            jax.ShapeDtypeStruct((tokens, width), jnp.float32),
            jax.ShapeDtypeStruct((tokens, width), jnp.float32),
            jax.ShapeDtypeStruct((tokens, 128), jnp.float32),
            jax.ShapeDtypeStruct((tokens, width), bf),
            jax.ShapeDtypeStruct((chunks, tokens, width), bf),
            *grad_shapes,
            jax.ShapeDtypeStruct((4 + chunks, width), jnp.float32),
        ],
        scratch_shapes=[
            pltpu.VMEM((chunks, tokens, width), bf),
            pltpu.VMEM((tokens, width), bf),
            pltpu.VMEM((chunks, rows, width), jnp.float32),
            *grad_scratch,
            *weight_scratch(sizes, width, chunks, True),
        ],
        compiler_params=pltpu.CompilerParams(vmem_limit_bytes=VMEM_LIMIT),
        cost_estimate=pl.CostEstimate(
            flops=2 * tokens * width * width * (1 + 4 * chunks),
            bytes_accessed=30 * 1024 * 1024,
            transcendentals=tokens * width * chunks,
        ),
        name="ffn",
    )(x, mixed, cot, vec, *weights, *deps)


def ffn_back_kernel(places, given, sum2_ref, n1_ref, rstd1_ref, gup_ref, vec_ref, *rest):
    weights, rest = rest[:given], rest[given:]
    sum1_ref, gatt_ref, gmix_ref, vsum_ref, wu_ref, wo_ref, load_ref = rest
    bf = jnp.bfloat16
    i = pl.program_id(0)
    width = sum2_ref.shape[1]

    @pl.when(i == 0)
    def _():
        copies = weight_copies(places, weights, None, wu_ref, wo_ref, load_ref)
        for copy in copies:
            copy.start()
        for copy in copies:
            copy.wait()

    ghid = sum2_ref[...]
    for j in range(wu_ref.shape[0]):
        ghid = ghid + nt_dot(gup_ref[j], wu_ref[j].reshape(width, width))
    n1 = n1_ref[...]
    sum1 = norm_back(ghid * vec_ref[1:2], n1, rstd1_ref[:, 0:1])
    sum1_ref[...] = sum1
    gatt = sum1.astype(bf)
    gatt_ref[...] = gatt
    gmix_ref[...] = nt_dot(gatt, wo_ref[...].reshape(width, width)).astype(bf)
    sums = jnp.concatenate(
        [
            jnp.sum(gatt.astype(jnp.float32), axis=0, keepdims=True),
            jnp.sum(ghid * n1, axis=0, keepdims=True),
            jnp.sum(ghid, axis=0, keepdims=True),
            jnp.zeros((5, width), jnp.float32),
        ],
        axis=0,
    )

    @pl.when(i == 0)
    def _():
        vsum_ref[...] = sums

    @pl.when(i > 0)
    def _():
        vsum_ref[...] += sums


def ffn_back(sum2, n1, rstd1, gup, vec, weights, places, sizes, rows, deps):
    bf = jnp.bfloat16
    tokens, width = sum2.shape
    chunks = gup.shape[0]
    block = pl.BlockSpec((rows, width), lambda i: (i, 0))
    return pl.pallas_call(
        partial(ffn_back_kernel, places, len(weights) + len(deps)),
        grid=(tokens // rows,),
        in_specs=[
            block,
            block,
            pl.BlockSpec((rows, 128), lambda i: (i, 0)),
            pl.BlockSpec((chunks, rows, width), lambda i: (0, i, 0)),
        ]
        + [const_spec(vec.shape)]
        + [ANY] * (len(weights) + len(deps)),
        out_specs=[block, block, block, const_spec((8, width))],
        out_shape=[
            jax.ShapeDtypeStruct((tokens, width), jnp.float32),
            jax.ShapeDtypeStruct((tokens, width), bf),
            jax.ShapeDtypeStruct((tokens, width), bf),
            jax.ShapeDtypeStruct((8, width), jnp.float32),
        ],
        scratch_shapes=weight_scratch(sizes, width, chunks, False),
        compiler_params=pltpu.CompilerParams(vmem_limit_bytes=VMEM_LIMIT),
        cost_estimate=pl.CostEstimate(
            flops=2 * tokens * width * width * (1 + chunks),
            bytes_accessed=20 * 1024 * 1024,
            transcendentals=0,
        ),
        name="ffn_back",
    )(sum2, n1, rstd1, gup, vec, *weights, *deps)


def weight_grad_kernel(split, given, where_ref, hid_ref, gup_ref, mixed_ref, gatt_ref, *rest):
    rest = rest[given:]
    bf = jnp.bfloat16
    i = pl.program_id(0)
    last = pl.num_programs(0) - 1
    if not split:
        dwu_ref, dwo_ref = rest
        dwu_ref[0] = tn_dot(hid_ref[...], gup_ref[0]).astype(bf)

        @pl.when(i == last)
        def _():
            dwo_ref[...] = tn_dot(mixed_ref[...], gatt_ref[...]).astype(bf)

        return
    mine_ref, theirs_ref, stage_ref, stage_out_ref, sem_ref, sem_out_ref = rest
    me, core = where_ref[0], where_ref[1]
    ns, nz, wr = stage_ref.shape[1:4]
    stage_ref[i] = tn_dot(hid_ref[...], gup_ref[0]).astype(bf).reshape(stage_ref.shape[1:])

    def up_copies(k, dst_ref):
        return [
            pltpu.make_async_copy(
                stage_ref.at[k, s], dst_ref.at[me ^ s, :, pl.ds((k % 2) * wr, wr)], sem_ref.at[k, s]
            )
            for s in range(ns)
        ]

    def out_copies():
        found = []
        for k, (dst_ref, half) in enumerate(((mine_ref, core), (theirs_ref, 1 - core))):
            cut = wr * 2 // 3
            for b in range(ns):
                found.append(
                    pltpu.make_async_copy(
                        stage_out_ref.at[half, b, :, pl.ds(0, cut)],
                        dst_ref.at[b, :, pl.ds(2 * wr, cut), pl.ds(0, stage_out_ref.shape[-1])],
                        sem_out_ref.at[k, b, 0],
                    )
                )
                found.append(
                    pltpu.make_async_copy(
                        stage_out_ref.at[half, b, :, pl.ds(cut, wr - cut)],
                        dst_ref.at[
                            b, :, pl.ds(2 * wr, wr - cut),
                            pl.ds(stage_out_ref.shape[-1], stage_out_ref.shape[-1]),
                        ],
                        sem_out_ref.at[k, b, 1],
                    )
                )
        return found

    for k in range(stage_ref.shape[0]):

        @pl.when(i == k)
        def _(k=k):
            for copy in up_copies(k, mine_ref if k < 2 else theirs_ref):
                copy.start()

    @pl.when(i == last)
    def _():
        grad = tn_dot(mixed_ref[...], gatt_ref[...]).astype(bf)
        lanes = stage_out_ref.shape[-1]
        for half in range(2):
            part = grad[:, half * lanes : (half + 1) * lanes]
            stage_out_ref[half] = part.reshape(stage_out_ref.shape[1:])
        out = out_copies()
        for copy in out:
            copy.start()
        for k in range(stage_ref.shape[0]):
            for copy in up_copies(k, mine_ref if k < 2 else theirs_ref):
                copy.wait()
        for copy in out:
            copy.wait()


def weight_grad(hid, gup, mixed, gatt, where, split, deps):
    bf = jnp.bfloat16
    chunks, tokens, width = gup.shape

    def const(shape):
        return pl.BlockSpec(shape, lambda i, w: (0,) * len(shape), pipeline_mode=pl.Buffered(1))

    if split:
        ns, nz, wr = split
        half = (ns, nz, 2 * wr + wr * 2 // 3, width)
        out_specs = [pl.BlockSpec(memory_space=pl.ANY)] * 2
        out_shape = [jax.ShapeDtypeStruct(half, bf)] * 2
        scratch = [
            pltpu.VMEM((chunks, ns, nz, wr, width), bf),
            pltpu.VMEM((2, ns, nz, wr, width // 2), bf),
            pltpu.SemaphoreType.DMA((chunks, ns)),
            pltpu.SemaphoreType.DMA((2, ns, 2)),
        ]
        up_map = lambda i, w: (lax.rem(2 * w[1] + i, chunks), 0, 0)
    else:
        out_specs = [pl.BlockSpec((1, width, width), lambda i, w: (i, 0, 0)), const((width, width))]
        out_shape = [
            jax.ShapeDtypeStruct((chunks, width, width), bf),
            jax.ShapeDtypeStruct((width, width), bf),
        ]
        scratch = []
        up_map = lambda i, w: (i, 0, 0)
    return pl.pallas_call(
        partial(weight_grad_kernel, bool(split), len(deps)),
        grid_spec=pltpu.PrefetchScalarGridSpec(
            num_scalar_prefetch=1,
            grid=(chunks,),
            in_specs=[
                const(hid.shape),
                pl.BlockSpec((1, tokens, width), up_map),
                const(mixed.shape),
                const(gatt.shape),
            ]
            + [ANY] * len(deps),
            out_specs=out_specs,
            scratch_shapes=scratch,
        ),
        out_shape=out_shape,
        compiler_params=pltpu.CompilerParams(vmem_limit_bytes=VMEM_LIMIT),
        cost_estimate=pl.CostEstimate(
            flops=2 * tokens * width * width * (1 + chunks),
            bytes_accessed=16 * 1024 * 1024,
            transcendentals=0,
        ),
        name="weight_grad",
    )(where, hid, gup, mixed, gatt, *deps)


def body(
    inputs,
    cotangent,
    lengths,
    query_weight,
    query_bias,
    key_weight,
    value_weight,
    value_bias,
    out_weight,
    out_bias,
    gain_one,
    shift_one,
    up_weight,
    up_bias,
    down_weight,
    down_bias,
    gain_two,
    shift_two,
):
    bf, f32 = jnp.bfloat16, jnp.float32
    seqs, rows, width = inputs.shape
    ns, nz, nc = lax.axis_size("seq"), lax.axis_size("zz"), lax.axis_size("core")
    nb = nz * nc
    n = ns * nb
    every = ("seq", "zz", "core")
    me = lax.axis_index("seq")
    core = lax.axis_index("core")
    length = rows * ns
    tokens = seqs * rows
    wr = query_weight.shape[0]
    ff = up_weight.shape[1]
    chunks = ff // width
    rd = down_weight.shape[0]
    hw = width // ns
    lanes = width // 2
    heads = hw // HEAD
    pair = 2 * wr
    cut = pair * 2 // 3
    aligned = pair % 48 == 0 and rd % 16 == 0 and chunks == ns

    def swap(a, bit):
        return lax.ppermute(a, "seq", [(i, i ^ bit) for i in range(ns)])

    def other_core(a):
        return lax.ppermute(a, "core", [(0, 1), (1, 0)])

    def pick(a, index, axis):
        return lax.dynamic_index_in_dim(a, index, axis, keepdims=False)

    def gather_seq(a):
        half = a.shape[0] // 2
        by_one, by_two = swap(a, 1), swap(a, 2)
        return [
            (0, 0, a),
            (1, 0, by_one),
            (2, 0, by_two),
            (3, 0, swap(by_one[:half], 2)),
            (3, half, swap(by_two[half:], 1)),
        ]

    def scatter_start(block_of, half):
        lo, hi = lambda b: block_of(b, 0, half), lambda b: block_of(b, half, 2 * half)
        return (
            swap(jnp.stack([lo(1), lo(3)]).astype(bf), 1),
            swap(jnp.stack([hi(2), hi(3)]).astype(bf), 2),
        )

    def scatter_next(block_of, half, got):
        lo, hi = lambda b: block_of(b, 0, half), lambda b: block_of(b, half, 2 * half)
        return (
            swap((lo(2) + got[0][1].astype(f32)).astype(bf), 2),
            swap((hi(1) + got[1][1].astype(f32)).astype(bf), 1),
        )

    def scatter_end(block_of, half, got, more):
        return jnp.concatenate(
            [
                block_of(0, 0, half) + got[0][0].astype(f32) + more[0].astype(f32),
                block_of(0, half, 2 * half) + got[1][0].astype(f32) + more[1].astype(f32),
            ],
            axis=0,
        )

    vectors = jnp.concatenate([out_bias, gain_one, shift_one, down_bias, gain_two, shift_two, up_bias])
    qkv_cols = jnp.concatenate(
        [w.reshape(wr, ns, hw).transpose(1, 0, 2) for w in (query_weight, key_weight, value_weight)], axis=2
    )
    early_rows = wr + 2 + (-(wr + 2) % 8)
    small = jnp.stack(
        [
            jnp.pad(jnp.concatenate([query_bias, value_bias]), (0, 3 * hw - pair)),
            jnp.pad(vectors, (0, 3 * hw - vectors.shape[0])),
        ]
    )
    small = jnp.pad(small, ((0, early_rows - wr - 2), (0, 0)))
    early = jnp.concatenate([qkv_cols, jnp.broadcast_to(small[None], (ns, *small.shape))], axis=1)
    early = jnp.broadcast_to(early[:, None], (ns, nb, early_rows, 3 * hw)).reshape(n, early_rows, 3 * hw)
    got = lax.all_to_all(early, every, 0, 0, tiled=True)
    weight_qkv = got[:, :wr].reshape(width, 3, hw)
    weight_qkv = jnp.pad(weight_qkv, ((0, 0), (0, 0), (0, LANES - hw))).reshape(width, 3 * LANES)
    bias_mine = lax.dynamic_slice_in_dim(got[:, wr], me * nb, nb, 0)
    ones = jnp.ones((LANES - hw,), bf)
    bias_qkv = jnp.concatenate(
        [
            bias_mine[:, :wr].reshape(hw),
            ones,
            jnp.zeros((LANES,), bf),
            bias_mine[:, wr:pair].reshape(hw),
            ones,
        ]
    ).astype(f32)
    vecs = got[:, wr + 1, : vectors.shape[0]].astype(f32)
    vec = jnp.concatenate(
        [
            vecs[:, : 6 * wr].reshape(n, 6, wr).transpose(1, 0, 2).reshape(6, width),
            vecs[:, 6 * wr :].reshape(chunks, width),
            jnp.zeros((6, width), f32),
        ]
    )[: 6 + chunks + (-(6 + chunks) % 8)]

    cols = jnp.concatenate([up_weight.reshape(wr, 2, 2 * width), out_weight.reshape(wr, 2, lanes)], axis=2)
    sent = other_core(pick(cols, 1 - core, 1))
    kept = pick(cols, core, 1)
    both = jnp.concatenate([jnp.where(core == 0, kept, sent), jnp.where(core == 0, sent, kept)], axis=0)
    both_out = both[:, 2 * width :]
    packed = jnp.concatenate(
        [
            down_weight,
            both[:, :width],
            both[:, width : 2 * width],
            jnp.concatenate([both_out[:cut], jnp.pad(both_out[cut:], ((0, 2 * cut - pair), (0, 0)))], axis=1),
        ],
        axis=0,
    )
    column = lax.all_gather(packed, "zz", axis=0, tiled=False)
    gathered = gather_seq(column)
    pieces, places = [], []
    for b, z, piece in gathered:
        places.append((b, z))
        pieces += [piece, other_core(piece)]
    waits = [[], [column], [gathered[1][2], gathered[2][2]]]
    if aligned:
        weights, places, sizes = pieces, tuple(places), (ns, nz, nc, rd, pair)
    else:
        halves = []
        for k in range(2):
            p = pieces[k::2]
            halves.append(jnp.stack([p[0], p[1], p[2], jnp.concatenate([p[3], p[4]], axis=0)]))
        rel = jnp.where(core == 0, jnp.stack(halves), jnp.stack(halves[::-1]))
        by_seq = jnp.stack([pick(rel, me ^ s, 1) for s in range(ns)], axis=1)
        whole_down = by_seq[:, :, :, :rd].transpose(1, 2, 0, 3, 4)
        whole_up = by_seq[:, :, :, rd : rd + 2 * pair].reshape(2, ns, nz, 2, pair, width).transpose(0, 3, 1, 2, 4, 5)
        folded = rel[:, :, :, rd + 2 * pair :]
        whole_out = jnp.concatenate([folded[..., :lanes], folded[:, :, :, : pair - cut, lanes:]], axis=3)
        whole_out = whole_out.transpose(1, 2, 3, 0, 4)
        whole = (chunks, width, width)
        weights = [whole_down.reshape(whole), whole_up.reshape(whole), whole_out.reshape(width, width)]
        places = sizes = None

    positions = ((me ^ jnp.arange(ns))[:, None] * rows + jnp.arange(rows)[None, :]).reshape(length)
    col = jnp.arange(3 * LANES, dtype=jnp.int32)
    seq_tokens, qkvs, mixes, stats, mixed_parts = [], [], [], [], []
    for j in range(seqs):
        whole = jnp.concatenate([block for _, _, block in gather_seq(inputs[j])], axis=0)
        qkv = (nn_dot(whole, weight_qkv) + bias_qkv).astype(bf)
        padding = jnp.where(positions < lengths[j], 0.0, NEG).astype(bf)
        qkv = jnp.where((col == LANES + hw)[None], padding[:, None], qkv)
        mix, stat = attend(qkv, heads, waits[j] if j < 3 else [])
        low = mix.astype(bf).reshape(ns, rows, hw)
        mixed_parts.append(jnp.concatenate([low[0]] + [swap(low[b], b) for b in range(1, ns)], axis=1))
        seq_tokens.append(whole)
        qkvs.append(qkv)
        mixes.append(mix)
        stats.append(stat)
    mixed = jnp.concatenate(mixed_parts, axis=0)

    x = inputs.reshape(tokens, width)
    output, sum2, n1, rstd1, hid, gup, *down_grads, vsum2 = ffn(
        x, mixed, cotangent.reshape(tokens, width), vec, weights, places, sizes, rows, chunks, []
    )
    def relative(a):
        return jnp.stack([pick(a, me ^ b, 0) for b in range(ns)])

    if not aligned:
        grad = relative(down_grads[0].reshape(ns, nz, 2, rd, width))
        down_grads = [pick(grad, core, 2), pick(grad, 1 - core, 2)]
    mine_down, got_down = down_grads[0], other_core(down_grads[1])
    half = nz // 2
    down_of = lambda b, lo, hi: mine_down[b, lo:hi].astype(f32) + got_down[b, lo:hi].astype(f32)
    sum1, gatt, gmix, vsum1 = ffn_back(
        sum2, n1, rstd1, gup, vec, weights if aligned else weights[1:], places, sizes, rows, []
    )
    gmix = gmix.reshape(seqs, rows, ns, hw)
    dos = [gmix[:, :, 0]] + [swap(gmix[:, :, b], b) for b in range(1, ns)]
    down_one = scatter_start(down_of, half)
    wide_grads = weight_grad(
        hid, gup, mixed, gatt, jnp.stack([me, core]).astype(jnp.int32), (ns, nz, pair) if aligned else None, [got_down]
    )
    if not aligned:
        up = wide_grads[0].reshape(2, 2, ns, nz, pair, width).transpose(2, 3, 0, 1, 4, 5)
        up = relative(up).reshape(ns, nz, 2, 2 * pair, width)
        out = wide_grads[1].reshape(ns, nz, pair, 2, lanes).transpose(0, 1, 3, 2, 4)
        out = jnp.concatenate(
            [out[..., :cut, :], jnp.pad(out[..., cut:, :], ((0, 0),) * 3 + ((0, 2 * cut - pair), (0, 0)))], axis=-1
        )
        grad = jnp.concatenate([up, out], axis=3)
        wide_grads = [pick(grad, core, 2), pick(grad, 1 - core, 2)]
    mine_wide, got_wide = wide_grads[0], other_core(wide_grads[1])
    wide_of = lambda b, lo, hi: mine_wide[b, lo:hi].astype(f32) + got_wide[b, lo:hi].astype(f32)

    down_two = scatter_next(down_of, half, down_one)
    wide_one = scatter_start(wide_of, half)
    wide_two = scatter_next(wide_of, half, wide_one)
    down_sum = scatter_end(down_of, half, down_one, down_two).astype(bf)
    wide_sum = scatter_end(wide_of, half, wide_one, wide_two).astype(bf)
    grad_down = lax.psum_scatter(down_sum, "zz", scatter_dimension=0, tiled=False).astype(f32)
    wide = lax.psum_scatter(wide_sum, "zz", scatter_dimension=0, tiled=False)
    waits = [[*down_one], [*down_two, got_wide], [*wide_one]]
    grad_qkvs, scatters = [], []
    for j in range(seqs):
        do = jnp.concatenate([d[j] for d in dos], axis=0)
        grad_qkv = attend_back(qkvs[j], mixes[j], do, stats[j], heads, waits[j] if j < 3 else [])
        parts = nt_dot(grad_qkv, weight_qkv).astype(bf).reshape(ns, rows, width)
        part_of = lambda b, lo, hi, parts=parts: parts[b, lo:hi].astype(f32)
        scatters.append((part_of, scatter_start(part_of, rows // 2)))
        grad_qkvs.append(grad_qkv)
    sum_qkv = jnp.zeros((width, 3 * LANES), f32)
    sum_bias = jnp.zeros((3 * LANES,), f32)
    for j in range(seqs):
        sum_qkv = sum_qkv + tn_dot(seq_tokens[j], grad_qkvs[j])
        sum_bias = sum_bias + jnp.sum(grad_qkvs[j].astype(f32), axis=0)
    grad_inputs = []
    for j in range(seqs):
        part_of, one = scatters[j]
        total = scatter_end(part_of, rows // 2, one, scatter_next(part_of, rows // 2, one))
        grad_inputs.append((sum1[j * rows : (j + 1) * rows] + total).astype(bf))
    grad_input = jnp.stack(grad_inputs)

    folded = wide[2 * pair :]
    both = jnp.concatenate(
        [wide[:pair], wide[pair : 2 * pair], jnp.concatenate([folded[:, :lanes], folded[: pair - cut, lanes:]], axis=0)],
        axis=1,
    ).reshape(2, wr, 2 * width + lanes)
    kept, sent = pick(both, core, 0), other_core(pick(both, 1 - core, 0))
    low_half, high_half = jnp.where(core == 0, kept, sent), jnp.where(core == 0, sent, kept)
    grad_up = jnp.concatenate([low_half[:, : 2 * width], high_half[:, : 2 * width]], axis=1).astype(f32)
    grad_out = jnp.concatenate([low_half[:, 2 * width :], high_half[:, 2 * width :]], axis=1).astype(f32)

    sum_qkv = sum_qkv.reshape(n, wr, 3, LANES)[..., :hw].reshape(n, wr, 3 * hw).astype(bf)
    bias_terms = jnp.concatenate(
        [sum_bias[:hw].reshape(nb, wr), sum_bias[2 * LANES : 2 * LANES + hw].reshape(nb, wr)], axis=1
    )
    bias_terms = jnp.pad(bias_terms, ((0, 0), (0, 3 * hw - pair)))
    bias_terms = jnp.broadcast_to(bias_terms[None], (ns, nb, 3 * hw)).reshape(n, 1, 3 * hw)
    vec_terms = jnp.concatenate([vsum1[:3], vsum2[:3]]).reshape(6, n, wr).transpose(1, 0, 2).reshape(n, 6 * wr)
    vec_terms = jnp.concatenate([vec_terms, vsum2[4:].reshape(n, rd)], axis=1)
    vec_terms = jnp.pad(vec_terms, ((0, 0), (0, 3 * hw - vec_terms.shape[1])))[:, None]
    back = jnp.concatenate(
        [sum_qkv, bias_terms.astype(bf), vec_terms.astype(bf), jnp.zeros((n, early_rows - wr - 2, 3 * hw), bf)], axis=1
    )
    back = lax.all_to_all(back, every, 0, 0, tiled=True)
    back = jnp.sum(back.reshape(ns, nb, early_rows, 3 * hw).astype(f32), axis=1)
    grads = back[:, :wr].reshape(ns, wr, 3, hw).transpose(2, 1, 0, 3).reshape(3, wr, width)
    bias_back = pick(back[:, wr], me, 0)
    vec_back = jnp.sum(back[:, wr + 1], axis=0)
    out_g, gain1_g, shift1_g, downb_g, gain2_g, shift2_g = (vec_back[i * wr : (i + 1) * wr] for i in range(6))
    return (
        output.reshape(seqs, rows, width),
        grad_input,
        grads[0],
        bias_back[:wr],
        grads[1],
        grads[2],
        bias_back[wr:pair],
        grad_out,
        out_g,
        gain1_g,
        shift1_g,
        grad_up,
        vec_back[6 * wr : 6 * wr + rd],
        grad_down,
        downb_g,
        gain2_g,
        shift2_g,
    )


def solution(mesh):
    sizes = mesh.shape
    cores = 2
    split = Mesh(
        mesh.devices.reshape(sizes["seq"], sizes["batch"] // cores, cores), ("seq", "zz", "core")
    )
    batch = ("zz", "core")
    every = ("seq", "zz", "core")
    tokens, matrix, vector = P(batch, "seq", None), P(every, None), P(every)
    return jax.shard_map(
        body,
        mesh=split,
        in_specs=(
            tokens, tokens, P(batch), matrix, vector, matrix, matrix, vector, matrix, vector,
            vector, vector, matrix, vector, matrix, vector, vector, vector,
        ),
        out_specs=(
            tokens, tokens, matrix, vector, matrix, matrix, vector, matrix, vector, vector,
            vector, matrix, vector, matrix, vector, vector, vector,
        ),
        check_vma=False,
    )
```

```python
from functools import partial

import jax
import jax.numpy as jnp
from jax import lax
from jax.experimental import pallas as pl
from jax.experimental.pallas import tpu as pltpu
from jax.sharding import Mesh
from jax.sharding import PartitionSpec as P

HEAD = 64
LANES = 256
SCALE = 0.125
LOG2E = 1.4426950408889634
NEG = -1e30
BRIEF = pl.CostEstimate(flops=1024, bytes_accessed=1024, transcendentals=0)
LONG = pl.CostEstimate(flops=20_000_000_000, bytes_accessed=1024, transcendentals=0)
VMEM_LIMIT = 56 * 1024 * 1024


def nt_dot(left, right):
    return lax.dot_general(left, right, (((1,), (1,)), ((), ())), preferred_element_type=jnp.float32)


def tn_dot(left, right):
    return lax.dot_general(left, right, (((0,), (0,)), ((), ())), preferred_element_type=jnp.float32)


def nn_dot(left, right):
    return jnp.dot(left, right, preferred_element_type=jnp.float32)


ANY = pl.BlockSpec(memory_space=pl.ANY)


def hint(index):
    return pl.multiple_of(index, 16)


def attend_kernel(heads, offset, scalars, own_ref, one_ref, two_ref, top_ref, bottom_ref, w_ref, bias_ref, *rest):
    bf = jnp.bfloat16
    qkv_ref, o_ref, stat_ref, wide_ref, mix_ref = rest[-5:]
    i, block = pl.program_id(0), pl.program_id(1)
    rows = own_ref.shape[1]
    width = heads * HEAD
    lane = lax.broadcasted_iota(jnp.int32, (1, LANES), 1)

    @pl.when((i == 0) & (block == 0))
    def _():
        zeros = jnp.zeros((w_ref.shape[0], LANES - width), bf)
        for t in range(3):
            wide_ref[:, t * LANES : t * LANES + width] = w_ref[:, t * width : (t + 1) * width]
            wide_ref[:, t * LANES + width : (t + 1) * LANES] = zeros

    @pl.when(block == 0)
    def _():
        me = scalars[0]
        for b, first, ref in (
            (0, 0, own_ref), (1, 0, one_ref), (2, 0, two_ref), (3, 0, top_ref), (3, rows // 2, bottom_ref)
        ):
            count = ref.shape[1]
            qkv = (nn_dot(ref[0], wide_ref[...]) + bias_ref[...]).astype(bf)
            at = (me ^ b) * rows + first + lax.broadcasted_iota(jnp.int32, (count, LANES), 0)
            padding = jnp.where(at < scalars[1 + offset + i], 0.0, NEG)
            key = jnp.where(lane == width, padding, qkv[:, LANES : 2 * LANES].astype(jnp.float32)).astype(bf)
            here = slice(b * rows + first, b * rows + first + count)
            qkv_ref[0, here, 0:LANES] = qkv[:, 0:LANES]
            qkv_ref[0, here, LANES : 2 * LANES] = key
            qkv_ref[0, here, 2 * LANES :] = qkv[:, 2 * LANES :]

    q = qkv_ref[0, pl.ds(hint(block * rows), rows), 0:LANES]
    total = jnp.zeros((rows, LANES), jnp.float32)
    stat = jnp.zeros((rows, 128), jnp.float32)
    lane_stat = lax.broadcasted_iota(jnp.int32, (1, 128), 1)
    for h in range(heads):
        own = lane // HEAD == h
        qh = jnp.where(own | (lane == width), q, jnp.zeros_like(q))
        s = nt_dot(qh, qkv_ref[0, :, LANES : 2 * LANES])
        top = jnp.max(s, axis=1, keepdims=True)
        p = jnp.exp2((s - top) * (SCALE * LOG2E))
        o = nn_dot(p.astype(bf), qkv_ref[0, :, 2 * LANES :])
        norm = o[:, width : width + 1]
        total = jnp.where(own, o * (1.0 / norm), total)
        stat = jnp.where(lane_stat == h, top * (SCALE * LOG2E) + jnp.log2(norm), stat)
    o_ref[0] = total[:, :width]
    stat_ref[0] = stat
    mix_ref[0, 0] = jnp.transpose(total)[:width].astype(bf)


def attend(scalars, first, seqs, pieces, w, bias, heads, deps):
    bf = jnp.bfloat16
    _, rows, width = pieces[0].shape
    length, mine = rows * 4, heads * HEAD
    whole = lambda shape: pl.BlockSpec(shape, lambda i, k, s: (0,) * len(shape), pipeline_mode=pl.Buffered(1))
    by_seq = lambda shape: pl.BlockSpec((1, *shape), lambda i, k, s: (i, 0, 0))
    by_block = lambda shape: pl.BlockSpec((1, *shape), lambda i, k, s: (i, k, 0))
    return pl.pallas_call(
        partial(attend_kernel, heads, first),
        grid_spec=pltpu.PrefetchScalarGridSpec(
            num_scalar_prefetch=1,
            grid=(seqs, 4),
            in_specs=[pl.BlockSpec((1, *p.shape[1:]), lambda i, k, s: (first + i, 0, 0)) for p in pieces]
            + [whole(w.shape), whole(bias.shape)]
            + [ANY] * len(deps),
            out_specs=[
                by_seq((length, 3 * LANES)),
                by_block((rows, mine)),
                by_block((rows, 128)),
                whole((width, 3 * LANES)),
            ]
            + [pl.BlockSpec((1, 1, mine, rows), lambda i, k, s: (s[0] ^ k, i, 0, 0))],
        ),
        out_shape=[
            jax.ShapeDtypeStruct((seqs, length, 3 * LANES), bf),
            jax.ShapeDtypeStruct((seqs, length, mine), jnp.float32),
            jax.ShapeDtypeStruct((seqs, length, 128), jnp.float32),
            jax.ShapeDtypeStruct((width, 3 * LANES), bf),
        ]
        + [jax.ShapeDtypeStruct((4, seqs, mine, rows), bf)],
        compiler_params=pltpu.CompilerParams(vmem_limit_bytes=VMEM_LIMIT),
        cost_estimate=BRIEF,
        name="attend",
    )(scalars, *pieces, w, bias, *deps)


def attend_back_kernel(heads, last, carried, qkv_ref, o_ref, stat_ref, *rest):
    bf = jnp.bfloat16
    dos_ref, piece_refs, (wide_ref, *rest) = rest[0], rest[1:6], rest[6:]
    before, rest = rest[:carried], rest[-9:]
    one_ref, two_ref, keep_ref, sum_ref, colsum_ref, dq_ref, rows_ref, do_ref, grad_ref = rest
    length = qkv_ref.shape[1]
    rows = dos_ref.shape[3]
    me = lax.axis_index("seq")
    width = heads * HEAD
    lane = lax.broadcasted_iota(jnp.int32, (1, LANES), 1)
    lane_w = lax.broadcasted_iota(jnp.int32, (1, width), 1)
    lane_stat = lax.broadcasted_iota(jnp.int32, (1, 128), 1)
    for b in range(4):
        do_ref[b * rows : (b + 1) * rows, :] = jnp.transpose(dos_ref[me ^ b, 0])
    prod = do_ref[...].astype(jnp.float32) * o_ref[0]
    stat = stat_ref[0]
    for h in range(heads):
        delta = jnp.sum(jnp.where(lane_w // HEAD == h, prod, 0.0), axis=1, keepdims=True)
        stat = jnp.where(lane_stat == heads + h, delta, stat)
    rows_ref[...] = jnp.transpose(stat)
    dq_ref[...] = jnp.zeros_like(dq_ref)

    def step(kb, carry):
        here = pl.ds(hint(kb * rows), rows)
        kblk = qkv_ref[0, here, LANES : 2 * LANES]
        vblk = qkv_ref[0, here, 2 * LANES : 2 * LANES + width]
        dk = jnp.zeros((rows, LANES), jnp.float32)
        dv = jnp.zeros((rows, width), jnp.float32)
        for h in range(heads):
            own = lane // HEAD == h
            own_w = lane_w // HEAD == h
            kh = jnp.where(own, kblk, jnp.zeros_like(kblk))
            kh_mask = jnp.where(own | (lane == width), kblk, jnp.zeros_like(kblk))
            vh = jnp.where(own_w, vblk, jnp.zeros_like(vblk))
            s = nt_dot(kh_mask, qkv_ref[0, :, 0:LANES])
            p = jnp.exp2(s * (SCALE * LOG2E) - rows_ref[h : h + 1, :])
            dp = nt_dot(vh, do_ref[...])
            ds = (p * (dp - rows_ref[heads + h : heads + h + 1, :])).astype(bf)
            dv = jnp.where(own_w, nn_dot(p.astype(bf), do_ref[...]), dv)
            dk = jnp.where(own, nn_dot(ds, qkv_ref[0, :, 0:LANES]), dk)
            dq_ref[...] += tn_dot(ds, kh)
        grad_ref[here, LANES : 2 * LANES] = (dk * SCALE).astype(bf)
        grad_ref[here, 2 * LANES : 2 * LANES + width] = dv.astype(bf)
        grad_ref[here, 2 * LANES + width :] = jnp.zeros((rows, LANES - width), bf)
        return carry

    lax.fori_loop(0, length // rows, step, 0)
    grad_ref[:, 0:LANES] = (dq_ref[...] * SCALE).astype(bf)

    half = rows // 2
    targets = {
        (0, 0): (keep_ref, 0), (1, 0): (one_ref, 0), (2, 0): (keep_ref, 1), (3, 0): (one_ref, 1),
        (0, 1): (keep_ref, 2), (1, 1): (keep_ref, 3), (2, 1): (two_ref, 0), (3, 1): (two_ref, 1),
    }
    for b in range(4):
        part = nt_dot(grad_ref[b * rows : (b + 1) * rows, :], wide_ref[...]).astype(bf)
        for upper in range(2):
            ref, at = targets[b, upper]
            ref[at] = part[upper * half : (upper + 1) * half]
    colsum = jnp.sum(grad_ref[...].astype(jnp.float32), axis=0, keepdims=True)
    total = None
    for first, ref in zip((0, rows, 2 * rows, 3 * rows, 3 * rows + half), piece_refs):
        term = tn_dot(ref[0], grad_ref[first : first + ref.shape[1], :])
        total = term if total is None else total + term
    if carried:
        total = total + before[0][...]
        colsum = colsum + before[1][0:1]
    colsum_ref[...] = jnp.broadcast_to(colsum, colsum_ref.shape)
    if last:
        for t in range(3):
            sum_ref[:, t * width : (t + 1) * width] = total[:, t * LANES : t * LANES + width].astype(bf)
    else:
        sum_ref[...] = total


def attend_back(j, local, last, qkv, o, stat, dos, pieces, wide, before, heads, deps):
    bf = jnp.bfloat16
    length, rows, width = qkv.shape[1], dos.shape[3], wide.shape[0]
    mine = heads * HEAD
    at = lambda index: lambda a: pl.BlockSpec((1, *a.shape[1:]), lambda i: (index, 0, 0))
    whole = lambda shape: pl.BlockSpec(shape, lambda i: (0,) * len(shape))
    outs = [
        ((2, rows // 2, width), bf),
        ((2, rows // 2, width), bf),
        ((4, rows // 2, width), bf),
        ((width, 3 * mine), bf) if last else ((width, 3 * LANES), jnp.float32),
        ((8, 3 * LANES), jnp.float32),
    ]
    return pl.pallas_call(
        partial(attend_back_kernel, heads, last, len(before)),
        grid=(1,),
        in_specs=[at(local)(a) for a in (qkv, o, stat)]
        + [pl.BlockSpec((4, 1, *dos.shape[2:]), lambda i: (0, j, 0, 0))]
        + [at(j)(a) for a in pieces]
        + [whole(a.shape) for a in (wide, *before)]
        + [ANY] * len(deps),
        out_specs=[whole(shape) for shape, _ in outs],
        out_shape=[jax.ShapeDtypeStruct(shape, kind) for shape, kind in outs],
        scratch_shapes=[
            pltpu.VMEM((length, LANES), jnp.float32),
            pltpu.VMEM((128, length), jnp.float32),
            pltpu.VMEM((length, mine), bf),
            pltpu.VMEM((length, 3 * LANES), bf),
        ],
        compiler_params=pltpu.CompilerParams(vmem_limit_bytes=VMEM_LIMIT),
        cost_estimate=LONG,
        name="attend_back",
    )(qkv, o, stat, dos, *pieces, wide, *before, *deps)


def weight_copies(places, refs, wd_ref, wu_ref, wo_ref, sem_ref):
    if places is None:
        pairs = list(zip(refs, [ref for ref in (wd_ref, wu_ref, wo_ref) if ref is not None]))
        return [pltpu.make_async_copy(a, d, sem_ref.at[q]) for q, (a, d) in enumerate(pairs)]
    me, core = lax.axis_index("seq"), lax.axis_index("core")
    rows_up, lanes = wo_ref.shape[2], wo_ref.shape[3] // 2
    cut = rows_up * 2 // 3
    pairs = []
    for p, (b, z) in enumerate(places):
        for k in range(2):
            src = refs[2 * p + k]
            base = src.shape[1] - cut
            down = base - 2 * rows_up
            c = core if k == 0 else 1 - core
            zs = pl.ds(z, src.shape[0])
            at = pl.multiple_of(c * lanes, 128)
            if wd_ref is not None:
                pairs.append((src.at[:, pl.ds(0, down)], wd_ref.at[me ^ b, zs, c]))
            pairs += [
                (src.at[:, pl.ds(down, rows_up)], wu_ref.at[2 * c, me ^ b, zs]),
                (src.at[:, pl.ds(down + rows_up, rows_up)], wu_ref.at[2 * c + 1, me ^ b, zs]),
                (
                    src.at[:, pl.ds(base, cut), pl.ds(0, lanes)],
                    wo_ref.at[b, zs, pl.ds(0, cut), pl.ds(at, lanes)],
                ),
                (
                    src.at[:, pl.ds(base, rows_up - cut), pl.ds(lanes, lanes)],
                    wo_ref.at[b, zs, pl.ds(cut, rows_up - cut), pl.ds(at, lanes)],
                ),
            ]
    return [pltpu.make_async_copy(a, d, sem_ref.at[q]) for q, (a, d) in enumerate(pairs)]


def weight_scratch(sizes, width, chunks, with_down):
    bf = jnp.bfloat16
    if sizes is None:
        shapes = [(chunks, width, width), (chunks, width, width), (width, width)]
    else:
        ns, nz, nc, rd, pair = sizes
        shapes = [(ns, nz, nc, rd, width), (chunks, ns, nz, pair, width), (ns, nz, pair, width)]
    return [pltpu.VMEM(s, bf) for s in shapes[0 if with_down else 1 :]] + [pltpu.SemaphoreType.DMA((64,))]


def normalise(r):
    mean = jnp.mean(r, axis=-1, keepdims=True)
    centred = r - mean
    rstd = lax.rsqrt(jnp.mean(centred * centred, axis=-1, keepdims=True) + 1e-05)
    return centred * rstd, rstd


def norm_back(e, n, rstd):
    return rstd * (e - jnp.mean(e, axis=-1, keepdims=True) - n * jnp.mean(e * n, axis=-1, keepdims=True))


GELU_A = 0.7978845608028654
GELU_B = 0.044715


def gelu_both(u):
    sq = u * u
    t = jnp.tanh(u * (GELU_A + (GELU_A * GELU_B) * sq))
    half = 0.5 * (1.0 + t)
    slope = half + (0.5 * u) * (1.0 - t * t) * (GELU_A + (3.0 * GELU_A * GELU_B) * sq)
    return u * half, slope


def ffn_kernel(
    places, given, early, x_ref, *rest
):
    split = places is not None
    mix_ref, mix_last_ref, cot_ref, vec_ref, *rest = rest
    weights, rest = rest[:given], rest[given:]
    out_ref, sum2_ref, n1_ref, rstd1_ref, hid_ref, gup_ref, mixed_ref, *rest = rest
    *rest, wd_ref, wu_ref, wo_ref, load_ref = rest
    if split:
        mine_ref, theirs_ref, vsum_ref, act_ref, gdl_ref, slope_ref, stage_ref, sem_ref = rest
    else:
        dwd_ref, vsum_ref, act_ref, gdl_ref, slope_ref = rest
    bf = jnp.bfloat16
    i = pl.program_id(0)
    rows, width = x_ref.shape
    chunks = wu_ref.shape[0]

    @pl.when(i == 0)
    def _():
        copies = weight_copies(places, weights, wd_ref, wu_ref, wo_ref, load_ref)
        for copy in copies:
            copy.start()
        for copy in copies:
            copy.wait()

    def wu(j):
        return wu_ref[j].reshape(width, width)

    def wd(j):
        return wd_ref[j].reshape(width, width)

    me = lax.axis_index("seq")
    mixed = [
        jnp.where(i < early, mix_ref[me ^ b, jnp.minimum(i, early - 1)], mix_last_ref[me ^ b, 0]) for b in range(4)
    ]
    mixed_ref[...] = jnp.transpose(jnp.concatenate(mixed, axis=0))
    vec = vec_ref[...]
    r = x_ref[...].astype(jnp.float32) + nn_dot(mixed_ref[...], wo_ref[...].reshape(width, width)) + vec[0:1]
    n1, rstd1 = normalise(r)
    n1_ref[...] = n1
    rstd1_ref[...] = jnp.broadcast_to(rstd1, rstd1_ref.shape)
    hidden = n1 * vec[1:2] + vec[2:3]
    hid_low = hidden.astype(bf)
    hid_ref[...] = hid_low
    mine = pl.ds(pl.multiple_of(i * rows, rows), rows)
    down = hidden + vec[3:4]
    for j in range(chunks):
        active, slope = gelu_both(nn_dot(hid_low, wu(j)) + vec[6 + j : 7 + j])
        slope_ref[j] = slope
        low = active.astype(bf)
        act_ref[j, mine, :] = low
        down = down + nn_dot(low, wd(j))
    n2, rstd2 = normalise(down)
    out_ref[...] = (n2 * vec[4:5] + vec[5:6]).astype(bf)
    cot = cot_ref[...].astype(jnp.float32)
    sum2 = norm_back(cot * vec[4:5], n2, rstd2)
    sum2_ref[...] = sum2
    gdl = sum2.astype(bf)
    gdl_ref[mine, :] = gdl
    sums = [
        jnp.sum(gdl.astype(jnp.float32), axis=0, keepdims=True),
        jnp.sum(cot * n2, axis=0, keepdims=True),
        jnp.sum(cot, axis=0, keepdims=True),
        jnp.zeros((1, width), jnp.float32),
    ]
    for j in range(chunks):
        gup = (nt_dot(gdl, wd(j)) * slope_ref[j]).astype(bf)
        gup_ref[j] = gup
        sums.append(jnp.sum(gup.astype(jnp.float32), axis=0, keepdims=True))
    sums = jnp.concatenate(sums, axis=0)

    @pl.when(i == 0)
    def _():
        vsum_ref[...] = sums

    @pl.when(i > 0)
    def _():
        vsum_ref[...] += sums

    @pl.when(i == pl.num_programs(0) - 1)
    def _():
        copies = []
        for j in range(chunks):
            grad = tn_dot(act_ref[j], gdl_ref[...]).astype(bf)
            if not split:
                dwd_ref[j] = grad
                continue
            stage_ref[j] = grad.reshape(stage_ref.shape[1:])
            core = lax.axis_index("core")
            for k, (dst_ref, half) in enumerate(((mine_ref, core), (theirs_ref, 1 - core))):
                copy = pltpu.make_async_copy(
                    stage_ref.at[j, :, half], dst_ref.at[me ^ j], sem_ref.at[j, k]
                )
                copy.start()
                copies.append(copy)
        for copy in copies:
            copy.wait()


def const_spec(shape):
    return pl.BlockSpec(shape, lambda i: (0,) * len(shape), pipeline_mode=pl.Buffered(1))


def ffn(x, mixed, cot, vec, weights, places, sizes, rows, chunks, deps):
    bf = jnp.bfloat16
    tokens, width = x.shape
    block = pl.BlockSpec((rows, width), lambda i: (i, 0))
    early = mixed[0].shape[1]
    if sizes:
        ns, nz, nc, wr, _ = sizes
        half = (ns, nz, wr, width)
        grad_specs = [pl.BlockSpec(memory_space=pl.ANY)] * 2
        grad_shapes = [jax.ShapeDtypeStruct(half, bf)] * 2
        grad_scratch = [
            pltpu.VMEM((chunks, nz, nc, wr, width), bf),
            pltpu.SemaphoreType.DMA((chunks, 2)),
        ]
    else:
        whole = (chunks, width, width)
        grad_specs, grad_shapes = [const_spec(whole)], [jax.ShapeDtypeStruct(whole, bf)]
        grad_scratch = []
    return pl.pallas_call(
        partial(ffn_kernel, places, len(weights) + len(deps), early),
        grid=(tokens // rows,),
        in_specs=[block]
        + [const_spec(m.shape) for m in mixed]
        + [block, const_spec(vec.shape)]
         + [ANY] * (len(weights) + len(deps)),
        out_specs=[
            block,
            block,
            block,
            pl.BlockSpec((rows, 128), lambda i: (i, 0)),
            block,
            pl.BlockSpec((chunks, rows, width), lambda i: (0, i, 0)),
            block,
            *grad_specs,
            const_spec((4 + chunks, width)),
        ],
        out_shape=[
            jax.ShapeDtypeStruct((tokens, width), bf),
            jax.ShapeDtypeStruct((tokens, width), jnp.float32),
            jax.ShapeDtypeStruct((tokens, width), jnp.float32),
            jax.ShapeDtypeStruct((tokens, 128), jnp.float32),
            jax.ShapeDtypeStruct((tokens, width), bf),
            jax.ShapeDtypeStruct((chunks, tokens, width), bf),
            jax.ShapeDtypeStruct((tokens, width), bf),
            *grad_shapes,
            jax.ShapeDtypeStruct((4 + chunks, width), jnp.float32),
        ],
        scratch_shapes=[
            pltpu.VMEM((chunks, tokens, width), bf),
            pltpu.VMEM((tokens, width), bf),
            pltpu.VMEM((chunks, rows, width), jnp.float32),
            *grad_scratch,
            *weight_scratch(sizes, width, chunks, True),
        ],
        compiler_params=pltpu.CompilerParams(vmem_limit_bytes=VMEM_LIMIT),
        cost_estimate=BRIEF,
        name="ffn",
    )(x, *mixed, cot, vec, *weights, *deps)


def ffn_back_kernel(places, given, sum2_ref, n1_ref, rstd1_ref, gup_ref, vec_ref, *rest):
    weights, rest = rest[:given], rest[given:]
    sum1_ref, gatt_ref, gmix_ref, vsum_ref, wu_ref, wo_ref, load_ref = rest
    bf = jnp.bfloat16
    i = pl.program_id(0)
    width = sum2_ref.shape[1]

    @pl.when(i == 0)
    def _():
        copies = weight_copies(places, weights, None, wu_ref, wo_ref, load_ref)
        for copy in copies:
            copy.start()
        for copy in copies:
            copy.wait()

    ghid = sum2_ref[...]
    for j in range(wu_ref.shape[0]):
        ghid = ghid + nt_dot(gup_ref[j], wu_ref[j].reshape(width, width))
    n1 = n1_ref[...]
    sum1 = norm_back(ghid * vec_ref[1:2], n1, rstd1_ref[:, 0:1])
    sum1_ref[...] = sum1
    gatt = sum1.astype(bf)
    gatt_ref[...] = gatt
    gmix = nt_dot(wo_ref[...].reshape(width, width), gatt).astype(bf)
    me = lax.axis_index("seq")
    for b in range(4):
        gmix_ref[me ^ b, 0] = gmix[b * (width // 4) : (b + 1) * (width // 4)]
    sums = jnp.concatenate(
        [
            jnp.sum(gatt.astype(jnp.float32), axis=0, keepdims=True),
            jnp.sum(ghid * n1, axis=0, keepdims=True),
            jnp.sum(ghid, axis=0, keepdims=True),
            jnp.zeros((5, width), jnp.float32),
        ],
        axis=0,
    )

    @pl.when(i == 0)
    def _():
        vsum_ref[...] = sums

    @pl.when(i > 0)
    def _():
        vsum_ref[...] += sums


def ffn_back(sum2, n1, rstd1, gup, vec, weights, places, sizes, rows, deps):
    bf = jnp.bfloat16
    tokens, width = sum2.shape
    chunks = gup.shape[0]
    block = pl.BlockSpec((rows, width), lambda i: (i, 0))
    return pl.pallas_call(
        partial(ffn_back_kernel, places, len(weights) + len(deps)),
        grid=(tokens // rows,),
        in_specs=[
            block,
            block,
            pl.BlockSpec((rows, 128), lambda i: (i, 0)),
            pl.BlockSpec((chunks, rows, width), lambda i: (0, i, 0)),
        ]
        + [const_spec(vec.shape)]
        + [ANY] * (len(weights) + len(deps)),
        out_specs=[block, block]
        + [pl.BlockSpec((4, 1, width // 4, rows), lambda i: (0, i, 0, 0))]
        + [const_spec((8, width))],
        out_shape=[
            jax.ShapeDtypeStruct((tokens, width), jnp.float32),
            jax.ShapeDtypeStruct((tokens, width), bf),
            jax.ShapeDtypeStruct((4, tokens // rows, width // 4, rows), bf),
            jax.ShapeDtypeStruct((8, width), jnp.float32),
        ],
        scratch_shapes=weight_scratch(sizes, width, chunks, False),
        compiler_params=pltpu.CompilerParams(vmem_limit_bytes=VMEM_LIMIT),
        cost_estimate=BRIEF,
        name="ffn_back",
    )(sum2, n1, rstd1, gup, vec, *weights, *deps)


def weight_grad_kernel(split, given, where_ref, hid_ref, gup_ref, mixed_ref, gatt_ref, *rest):
    rest = rest[given:]
    bf = jnp.bfloat16
    i = pl.program_id(0)
    last = pl.num_programs(0) - 1
    if not split:
        dwu_ref, dwo_ref = rest
        dwu_ref[0] = tn_dot(hid_ref[...], gup_ref[0]).astype(bf)

        @pl.when(i == last)
        def _():
            dwo_ref[...] = tn_dot(mixed_ref[...], gatt_ref[...]).astype(bf)

        return
    mine_ref, theirs_ref, stage_ref, stage_out_ref, sem_ref, sem_out_ref = rest
    me, core = where_ref[0], where_ref[1]
    ns, nz, wr = stage_ref.shape[1:4]
    stage_ref[i] = tn_dot(hid_ref[...], gup_ref[0]).astype(bf).reshape(stage_ref.shape[1:])

    def up_copies(k, dst_ref):
        return [
            pltpu.make_async_copy(
                stage_ref.at[k, s], dst_ref.at[me ^ s, :, pl.ds((k % 2) * wr, wr)], sem_ref.at[k, s]
            )
            for s in range(ns)
        ]

    def out_copies():
        found = []
        for k, (dst_ref, half) in enumerate(((mine_ref, core), (theirs_ref, 1 - core))):
            cut = wr * 2 // 3
            for b in range(ns):
                found.append(
                    pltpu.make_async_copy(
                        stage_out_ref.at[half, b, :, pl.ds(0, cut)],
                        dst_ref.at[b, :, pl.ds(2 * wr, cut), pl.ds(0, stage_out_ref.shape[-1])],
                        sem_out_ref.at[k, b, 0],
                    )
                )
                found.append(
                    pltpu.make_async_copy(
                        stage_out_ref.at[half, b, :, pl.ds(cut, wr - cut)],
                        dst_ref.at[
                            b, :, pl.ds(2 * wr, wr - cut),
                            pl.ds(stage_out_ref.shape[-1], stage_out_ref.shape[-1]),
                        ],
                        sem_out_ref.at[k, b, 1],
                    )
                )
        return found

    for k in range(stage_ref.shape[0]):

        @pl.when(i == k)
        def _(k=k):
            for copy in up_copies(k, mine_ref if k < 2 else theirs_ref):
                copy.start()

    @pl.when(i == last)
    def _():
        grad = tn_dot(mixed_ref[...], gatt_ref[...]).astype(bf)
        lanes = stage_out_ref.shape[-1]
        for half in range(2):
            part = grad[:, half * lanes : (half + 1) * lanes]
            stage_out_ref[half] = part.reshape(stage_out_ref.shape[1:])
        out = out_copies()
        for copy in out:
            copy.start()
        for k in range(stage_ref.shape[0]):
            for copy in up_copies(k, mine_ref if k < 2 else theirs_ref):
                copy.wait()
        for copy in out:
            copy.wait()


def weight_grad(hid, gup, mixed, gatt, where, split, deps):
    bf = jnp.bfloat16
    chunks, tokens, width = gup.shape

    def const(shape):
        return pl.BlockSpec(shape, lambda i, w: (0,) * len(shape), pipeline_mode=pl.Buffered(1))

    if split:
        ns, nz, wr = split
        half = (ns, nz, 2 * wr + wr * 2 // 3, width)
        out_specs = [pl.BlockSpec(memory_space=pl.ANY)] * 2
        out_shape = [jax.ShapeDtypeStruct(half, bf)] * 2
        scratch = [
            pltpu.VMEM((chunks, ns, nz, wr, width), bf),
            pltpu.VMEM((2, ns, nz, wr, width // 2), bf),
            pltpu.SemaphoreType.DMA((chunks, ns)),
            pltpu.SemaphoreType.DMA((2, ns, 2)),
        ]
        up_map = lambda i, w: (lax.rem(2 * w[1] + i, chunks), 0, 0)
    else:
        out_specs = [pl.BlockSpec((1, width, width), lambda i, w: (i, 0, 0)), const((width, width))]
        out_shape = [
            jax.ShapeDtypeStruct((chunks, width, width), bf),
            jax.ShapeDtypeStruct((width, width), bf),
        ]
        scratch = []
        up_map = lambda i, w: (i, 0, 0)
    return pl.pallas_call(
        partial(weight_grad_kernel, bool(split), len(deps)),
        grid_spec=pltpu.PrefetchScalarGridSpec(
            num_scalar_prefetch=1,
            grid=(chunks,),
            in_specs=[
                const(hid.shape),
                pl.BlockSpec((1, tokens, width), up_map),
                const(mixed.shape),
                const(gatt.shape),
            ]
            + [ANY] * len(deps),
            out_specs=out_specs,
            scratch_shapes=scratch,
        ),
        out_shape=out_shape,
        compiler_params=pltpu.CompilerParams(vmem_limit_bytes=VMEM_LIMIT),
        cost_estimate=BRIEF,
        name="weight_grad",
    )(where, hid, gup, mixed, gatt, *deps)


def body(
    inputs,
    cotangent,
    lengths,
    query_weight,
    query_bias,
    key_weight,
    value_weight,
    value_bias,
    out_weight,
    out_bias,
    gain_one,
    shift_one,
    up_weight,
    up_bias,
    down_weight,
    down_bias,
    gain_two,
    shift_two,
):
    bf, f32 = jnp.bfloat16, jnp.float32
    seqs, rows, width = inputs.shape
    ns, nz, nc = lax.axis_size("seq"), lax.axis_size("zz"), lax.axis_size("core")
    nb = nz * nc
    n = ns * nb
    every = ("seq", "zz", "core")
    me = lax.axis_index("seq")
    core = lax.axis_index("core")
    length = rows * ns
    tokens = seqs * rows
    wr = query_weight.shape[0]
    ff = up_weight.shape[1]
    chunks = ff // width
    rd = down_weight.shape[0]
    hw = width // ns
    lanes = width // 2
    heads = hw // HEAD
    pair = 2 * wr
    cut = pair * 2 // 3
    aligned = pair % 48 == 0 and rd % 16 == 0 and chunks == ns

    def swap(a, bit):
        return lax.ppermute(a, "seq", [(i, i ^ bit) for i in range(ns)])

    def other_core(a):
        return lax.ppermute(a, "core", [(0, 1), (1, 0)])

    def after(a, *deps):
        return lax.optimization_barrier((a, deps))[0]

    def pick(a, index, axis):
        return lax.dynamic_index_in_dim(a, index, axis, keepdims=False)

    def scatter_start(block_of, half):
        lo, hi = lambda b: block_of(b, 0, half), lambda b: block_of(b, half, 2 * half)
        return (
            swap(jnp.stack([lo(1), lo(3)]).astype(bf), 1),
            swap(jnp.stack([hi(2), hi(3)]).astype(bf), 2),
        )

    def scatter_next(block_of, half, got):
        lo, hi = lambda b: block_of(b, 0, half), lambda b: block_of(b, half, 2 * half)
        return (
            swap((lo(2) + got[0][1].astype(f32)).astype(bf), 2),
            swap((hi(1) + got[1][1].astype(f32)).astype(bf), 1),
        )

    def scatter_end(block_of, half, got, more):
        return jnp.concatenate(
            [
                block_of(0, 0, half) + got[0][0].astype(f32) + more[0].astype(f32),
                block_of(0, half, 2 * half) + got[1][0].astype(f32) + more[1].astype(f32),
            ],
            axis=0,
        )

    cols = jnp.concatenate([up_weight.reshape(wr, 2, 2 * width), out_weight.reshape(wr, 2, lanes)], axis=2)
    sent = other_core(pick(cols, 1 - core, 1))
    kept = pick(cols, core, 1)
    both = jnp.concatenate([jnp.where(core == 0, kept, sent), jnp.where(core == 0, sent, kept)], axis=0)
    both_out = both[:, 2 * width :]
    packed = jnp.concatenate(
        [
            down_weight,
            both[:, :width],
            both[:, width : 2 * width],
            jnp.concatenate([both_out[:cut], jnp.pad(both_out[cut:], ((0, 2 * cut - pair), (0, 0)))], axis=1),
        ],
        axis=0,
    )
    column = lax.all_gather(packed, "zz", axis=0, tiled=False)
    vectors = jnp.concatenate(
        [
            jnp.stack([out_bias, gain_one, shift_one, down_bias, gain_two, shift_two, query_bias, value_bias]),
            up_bias.reshape(chunks, wr),
        ]
    )
    wide_cols = 3 * hw + 64
    qkv_cols = jnp.concatenate(
        [w.reshape(wr, ns, hw).transpose(1, 0, 2) for w in (query_weight, key_weight, value_weight)]
        + [jnp.broadcast_to(jnp.pad(vectors.T, ((0, 0), (0, 64 - 8 - chunks)))[None], (ns, wr, 64))],
        axis=2,
    )
    early = jnp.broadcast_to(qkv_cols[:, None], (ns, nb, wr, wide_cols)).reshape(n, wr, wide_cols)
    got = lax.all_to_all(early, every, 0, 0, tiled=True).reshape(width, wide_cols)
    weight_qkv = got[:, : 3 * hw]
    rows_of = got[:, 3 * hw :].astype(f32).T
    ones = jnp.ones((LANES - hw,), f32)
    bias_qkv = jnp.concatenate(
        [
            lax.dynamic_slice_in_dim(rows_of[6], me * hw, hw, 0),
            ones,
            jnp.zeros((LANES,), f32),
            lax.dynamic_slice_in_dim(rows_of[7], me * hw, hw, 0),
            ones,
        ]
    )[None]
    bias_up = rows_of[8 : 8 + chunks].reshape(chunks, n, wr).transpose(1, 0, 2).reshape(chunks, width)
    vec = jnp.concatenate([rows_of[:6], bias_up, jnp.zeros(((-(6 + chunks)) % 8, width), f32)])

    half = rows // 2
    by_one, by_two = swap(inputs, 1), swap(inputs, 2)
    blocks = [inputs, by_one, by_two, swap(by_one[:, :half], 2), swap(by_two[:, half:], 1)]
    column = after(column, got, *blocks)
    column_one, column_two = swap(column, 1), swap(column, 2)
    scalars = jnp.concatenate([me[None], lengths]).astype(jnp.int32)
    early = seqs - 1
    calls, mixed = [], []
    for first, count, deps in ((0, early, [column]), (early, 1, [column_one, column_two])):
        qkv, mix, stat, wide_qkv, part = attend(
            scalars, first, count, blocks, weight_qkv, bias_qkv, heads, deps + [c[0] for c in calls]
        )
        calls.append((qkv, mix, stat))
        mixed.append(lax.all_to_all(part, "seq", 0, 0, tiled=True))
        if first == 0:
            column_one, column_two = after((column_one, column_two), qkv)
            top, bottom = swap(column_one[: nz // 2], 2), swap(column_two[nz // 2 :], 1)

    top, bottom = after((top, bottom), calls[1][0])
    gathered = [(0, 0, column), (1, 0, column_one), (2, 0, column_two), (3, 0, top), (3, nz // 2, bottom)]
    pieces, places = [], []
    for b, z, piece in gathered:
        places.append((b, z))
        pieces += [piece, other_core(piece)]
    if aligned:
        weights, places, sizes = pieces, tuple(places), (ns, nz, nc, rd, pair)
    else:
        halves = []
        for k in range(2):
            p = pieces[k::2]
            halves.append(jnp.stack([p[0], p[1], p[2], jnp.concatenate([p[3], p[4]], axis=0)]))
        rel = jnp.where(core == 0, jnp.stack(halves), jnp.stack(halves[::-1]))
        by_seq = jnp.stack([pick(rel, me ^ s, 1) for s in range(ns)], axis=1)
        whole_down = by_seq[:, :, :, :rd].transpose(1, 2, 0, 3, 4)
        whole_up = by_seq[:, :, :, rd : rd + 2 * pair].reshape(2, ns, nz, 2, pair, width).transpose(0, 3, 1, 2, 4, 5)
        folded = rel[:, :, :, rd + 2 * pair :]
        whole_out = jnp.concatenate([folded[..., :lanes], folded[:, :, :, : pair - cut, lanes:]], axis=3)
        whole_out = whole_out.transpose(1, 2, 3, 0, 4)
        whole = (chunks, width, width)
        weights = [whole_down.reshape(whole), whole_up.reshape(whole), whole_out.reshape(width, width)]
        places = sizes = None

    x = inputs.reshape(tokens, width)
    output, sum2, n1, rstd1, hid, gup, mixed, *down_grads, vsum2 = ffn(
        x, mixed, cotangent.reshape(tokens, width), vec, weights, places, sizes, rows, chunks, []
    )
    def relative(a):
        return jnp.stack([pick(a, me ^ b, 0) for b in range(ns)])

    if not aligned:
        grad = relative(down_grads[0].reshape(ns, nz, 2, rd, width))
        down_grads = [pick(grad, core, 2), pick(grad, 1 - core, 2)]
    mine_down, got_down = down_grads[0], other_core(down_grads[1])
    zhalf = nz // 2
    down_of = lambda b, lo, hi: mine_down[b, lo:hi].astype(f32) + got_down[b, lo:hi].astype(f32)
    sum1, gatt, gmix, vsum1 = ffn_back(
        sum2, n1, rstd1, gup, vec, weights if aligned else weights[1:], places, sizes, rows, []
    )
    dos = lax.all_to_all(gmix, "seq", 0, 0, tiled=True)
    down_one = scatter_start(down_of, zhalf)
    wide_grads = weight_grad(
        hid, gup, mixed, gatt, jnp.stack([me, core]).astype(jnp.int32), (ns, nz, pair) if aligned else None, [got_down]
    )
    if not aligned:
        up = wide_grads[0].reshape(2, 2, ns, nz, pair, width).transpose(2, 3, 0, 1, 4, 5)
        up = relative(up).reshape(ns, nz, 2, 2 * pair, width)
        out = wide_grads[1].reshape(ns, nz, pair, 2, lanes).transpose(0, 1, 3, 2, 4)
        out = jnp.concatenate(
            [out[..., :cut, :], jnp.pad(out[..., cut:, :], ((0, 0),) * 3 + ((0, 2 * cut - pair), (0, 0)))], axis=-1
        )
        grad = jnp.concatenate([up, out], axis=3)
        wide_grads = [pick(grad, core, 2), pick(grad, 1 - core, 2)]
    mine_wide, theirs_wide = wide_grads
    dos = after(dos, mine_wide)

    kept, ones, twos, grad_inputs = [], [], [], []
    got_wide = other_core(theirs_wide)
    down_two = scatter_next(down_of, zhalf, down_one)
    wide_of = lambda b, lo, hi: mine_wide[b, lo:hi].astype(f32) + got_wide[b, lo:hi].astype(f32)
    wide_one = scatter_start(wide_of, zhalf)
    wide_two = scatter_next(wide_of, zhalf, wide_one)
    wide_sum = scatter_end(wide_of, zhalf, wide_one, wide_two).astype(bf)
    before, sends = [], []
    for j, waits in enumerate(([], [*down_one, got_wide], [*down_two, *wide_one])):
        send_one, send_two, keep, *before = attend_back(
            j, j % early, j == seqs - 1, *calls[j // early], dos, blocks, wide_qkv, before, heads, waits
        )
        if j == 1:
            down_sum = scatter_end(down_of, zhalf, down_one, after(down_two, keep)).astype(bf)
        if j > 1:
            ones[-1] = after(ones[-1], keep)
        if j:
            sent_one, sent_two = after(sends[-1], keep)
            ones.append((swap(sent_one, 1), swap(sent_two, 2)))
        sends.append((send_one, send_two))
        kept.append(keep)
    ones.append((swap(send_one, 1), swap(send_two, 2)))
    sum_qkv, sum_bias = before
    for j in range(seqs):
        keep, (one, two) = kept[j].astype(f32), ones[j]
        low = swap((keep[1] + one[1].astype(f32)).astype(bf), 2)
        high = swap((keep[3] + two[1].astype(f32)).astype(bf), 1)
        low, high = keep[0] + one[0].astype(f32) + low.astype(f32), keep[2] + two[0].astype(f32) + high.astype(f32)
        total = sum1[j * rows : (j + 1) * rows] + jnp.concatenate([low, high], axis=0)
        grad_inputs.append(total.astype(bf))
    grad_input = jnp.stack(grad_inputs)
    grad_down = lax.psum_scatter(down_sum, "zz", scatter_dimension=0, tiled=False)
    grad_down = after(grad_down, sum_qkv).astype(f32)
    wide = after(lax.psum_scatter(wide_sum, "zz", scatter_dimension=0, tiled=False), sum_qkv)

    folded = wide[2 * pair :]
    both = jnp.concatenate(
        [wide[:pair], wide[pair : 2 * pair], jnp.concatenate([folded[:, :lanes], folded[: pair - cut, lanes:]], axis=0)],
        axis=1,
    ).reshape(2, wr, 2 * width + lanes)
    kept, sent = pick(both, core, 0), other_core(pick(both, 1 - core, 0))
    low_half, high_half = jnp.where(core == 0, kept, sent), jnp.where(core == 0, sent, kept)
    grad_up = jnp.concatenate([low_half[:, : 2 * width], high_half[:, : 2 * width]], axis=1).astype(f32)
    grad_out = jnp.concatenate([low_half[:, 2 * width :], high_half[:, 2 * width :]], axis=1).astype(f32)

    zero_row = jnp.zeros((width,), f32)
    bias_rows = [
        lax.dynamic_update_slice_in_dim(zero_row, sum_bias[0, t * LANES : t * LANES + hw], me * hw, 0) for t in (0, 2)
    ]
    rows_back = jnp.concatenate(
        [
            vsum1[:3],
            vsum2[:3],
            jnp.stack(bias_rows),
            vsum2[4:].reshape(n, chunks, wr).transpose(1, 0, 2).reshape(chunks, width),
            jnp.zeros((64 - 8 - chunks, width), f32),
        ]
    )
    back = jnp.concatenate([sum_qkv, rows_back.T.astype(bf)], axis=1).reshape(n, wr, wide_cols)
    back = lax.all_to_all(back, every, 0, 0, tiled=True)
    back = jnp.sum(back.reshape(ns, nb, wr, wide_cols).astype(f32), axis=1)
    grads = back[..., : 3 * hw].reshape(ns, wr, 3, hw).transpose(2, 1, 0, 3).reshape(3, wr, width)
    rows_back = jnp.sum(back[..., 3 * hw :], axis=0).T
    out_g, gain1_g, shift1_g, downb_g, gain2_g, shift2_g, query_g, value_g = (rows_back[i] for i in range(8))
    return (
        output.reshape(seqs, rows, width),
        grad_input,
        grads[0],
        query_g,
        grads[1],
        grads[2],
        value_g,
        grad_out,
        out_g,
        gain1_g,
        shift1_g,
        grad_up,
        rows_back[8 : 8 + chunks].reshape(rd),
        grad_down,
        downb_g,
        gain2_g,
        shift2_g,
    )


def solution(mesh):
    sizes = mesh.shape
    cores = 2
    split = Mesh(
        mesh.devices.reshape(sizes["seq"], sizes["batch"] // cores, cores), ("seq", "zz", "core")
    )
    batch = ("zz", "core")
    every = ("seq", "zz", "core")
    tokens, matrix, vector = P(batch, "seq", None), P(every, None), P(every)
    return jax.shard_map(
        body,
        mesh=split,
        in_specs=(
            tokens, tokens, P(batch), matrix, vector, matrix, matrix, vector, matrix, vector,
            vector, vector, matrix, vector, matrix, vector, vector, vector,
        ),
        out_specs=(
            tokens, tokens, matrix, vector, matrix, matrix, vector, matrix, vector, vector,
            vector, matrix, vector, matrix, vector, vector, vector,
        ),
        check_vma=False,
    )
```
